128 devices in a mesh: seq: 16 (over y, x_lo, core), tensor: 8 (over z, x_hi).
Axes of the slice: x: 4 (x_hi: 2, x_lo: 2; x = x_hi * 2 + x_lo), y: 4, z: 4, core: 2. Of those that a mesh axis runs over, the one named last changes fastest.
Arguments:
- tokens: bfloat16 [2048, 16384], P('seq', 'tensor'), may hold values from -100 to 100
- norm_gain: float32 [16384], P('tensor'), may hold values from 0.5 to 1.5
- projection_weight: bfloat16 [2048, 16384], P('tensor', 'seq'), may hold values from -1.5 to 1.5
- panel_index: int32 [1], replicated, may hold values from 0 to 31
Outputs:
- gram: float32 [16384, 16384], P('seq', 'tensor')
- factor_panel: bfloat16 [16384, 512], P('seq')
- projected: float32 [2048, 512], P('tensor', 'seq')
The draws below stay inside these ranges and needn't reach their ends.
All inputs are finite; a program needn't handle non-finite values.
Results may differ from the reference program's by a relative error of at most 0.0057.
Values may be sent and summed in bfloat16 or wider, within the bound.
A program may use at most 128 MiB of HBM per device.

```python
import math
import jax
import jax.numpy as jnp
from jax import lax

D = 16384
PANEL = 512
TOKENS = 2048
KV_ROWS = 2048
NPANELS = 32


def draw_tokens(key, part):
    first, second = jax.random.split(key, 2)
    position = jnp.arange(D, dtype=jnp.float32) / D
    token_place = jnp.arange(TOKENS, dtype=jnp.float32)[:, None] / TOKENS
    values = jax.random.normal(first, (TOKENS, D), jnp.float32)
    row_scale = jnp.exp(math.log(10.0) * (-3.0 + 2.0 * token_place))
    values = values * row_scale
    rising = jnp.exp(0.5 * math.log(3.0) * position)
    rough = jax.random.uniform(second, (1, D), jnp.float32, 0.5, 1.5)
    result = jnp.clip(values * rough * rising[None, :], -100.0, 100.0)
    return result.astype(jnp.bfloat16)


def level_of(stream_key, shape, cuts, least, largest):
    gain, own = 1.0, jax.random.fold_in(stream_key, 6)
    for axis_at, parts in cuts:
        heights = jnp.exp(jax.random.uniform(jax.random.fold_in(own, axis_at), (parts,), jnp.float32, least / len(cuts), largest / len(cuts)))
        gain = gain * jnp.repeat(heights, shape[axis_at] // parts).reshape([-1 if axis == axis_at else 1 for axis in range(len(shape))])
    return gain


def normal_values(own_key, extent, scale, reach, cuts=(), held_as=jnp.bfloat16):
    values = scale * jax.random.normal(own_key, extent, jnp.float32)
    if cuts:
        values = values * level_of(own_key, extent, cuts, -0.22, 0.18)
    return jnp.clip(values, -reach, reach).astype(held_as)


def setup_inputs(seed: int = 0) -> dict:
    keys = jax.random.split(jax.random.key(seed), 5)
    tokens = draw_tokens(jax.random.fold_in(keys[4], 71), 0)
    norm_gain = jnp.clip(1.0 + 0.1 * jax.random.normal(keys[1], (D,), jnp.float32), 0.5, 1.5)
    projection_weight = normal_values(keys[2], (KV_ROWS, D), 0.25, 1.5, ((0, 8), (1, 16)))
    panel_index = jax.random.randint(keys[3], (1,), 0, NPANELS).astype(jnp.int32)
    return {"tokens": tokens, "norm_gain": norm_gain, "projection_weight": projection_weight, "panel_index": panel_index}


epsilon = 1e-05
damping = 0.1

def reference(tokens, norm_gain, projection_weight, panel_index):
    token_values = tokens.astype(jnp.float32)
    squares = lax.optimization_barrier(jnp.sum(token_values * token_values, axis=1, keepdims=True))
    normed = (token_values * lax.rsqrt(squares / D + epsilon) * norm_gain[None, :]).astype(jnp.bfloat16)
    normed_wide = normed.astype(jnp.float32)
    gram = jnp.dot(normed_wide.T, normed_wide, precision=lax.Precision.HIGHEST) / TOKENS
    trace_sum = jnp.sum(normed_wide * normed_wide) / TOKENS
    diag_shift = damping * trace_sum / D
    diag_ids = jnp.arange(D, dtype=jnp.int32)
    gram = gram.at[diag_ids, diag_ids].add(diag_shift)
    panel_start = (panel_index[0] * PANEL).astype(jnp.int32)
    panel_cols = lax.dynamic_slice_in_dim(gram, panel_start, PANEL, 1)
    diag_block = lax.dynamic_slice_in_dim(panel_cols, panel_start, PANEL, 0)
    factor = jnp.linalg.cholesky(diag_block)
    whitened = lax.linalg.triangular_solve(factor, panel_cols, left_side=False, lower=True, transpose_a=True)
    factor_panel = whitened.astype(jnp.bfloat16)
    projected = jnp.dot(projection_weight.astype(jnp.float32), factor_panel.astype(jnp.float32), preferred_element_type=jnp.float32)
    return (gram, factor_panel, projected)
```

```python
import functools

import jax
import jax.numpy as jnp
from jax import lax
from jax.experimental import pallas as pl
from jax.experimental.pallas import tpu as pltpu
from jax.sharding import PartitionSpec as P

D = 16384
PANEL = 512
TOKENS = 2048
EPSILON = 1e-05
DAMPING = 0.1
F32 = jnp.float32
BF16 = jnp.bfloat16
MESH = pl.DeviceIdType.MESH


def halves(a):
    high = a.astype(BF16)
    return high, (a - high.astype(F32)).astype(BF16)


def dot(a, b, dims):
    return lax.dot_general(a, b, (dims, ((), ())), preferred_element_type=F32)


def dot_split(a, b, dims):
    ah, al = halves(a)
    bh, bl = halves(b)
    return dot(ah, bh, dims) + (dot(ah, bl, dims) + dot(al, bh, dims))


def row_of(tile, r):
    return jnp.broadcast_to(tile[r : r + 1, :], (8, 128))


def column_of(tile, k):
    return jnp.broadcast_to(tile[:, k : k + 1], (8, 128))


def inverse_factor(a):
    sub = lax.broadcasted_iota(jnp.int32, (8, 128), 0)
    lane = lax.broadcasted_iota(jnp.int32, (8, 128), 1)
    inv = [jnp.where(sub + 8 * g == lane, 1.0, 0.0).astype(F32) for g in range(16)]
    for g in range(16):
        cols = [{k: column_of(a[k], 8 * g + c) for k in range(g, 16)} for c in range(8)]
        for c in range(8):
            r = lax.rsqrt(row_of(cols[c][g], c))
            m = {k: cols[c][k] * r for k in range(g, 16)}
            for c2 in range(c + 1, 8):
                f = row_of(cols[c2][g], c) * r
                for k in range(g, 16):
                    cols[c2][k] = cols[c2][k] - m[k] * f
            u = row_of(a[g], c) * r
            z = row_of(inv[g], c) * r
            m[g] = jnp.where(sub > c, m[g], 0.0)
            for k in range(g, 16):
                a[k] = a[k] - m[k] * u
                inv[k] = inv[k] - m[k] * z
            inv[g] = jnp.where(sub == c, z, inv[g])
    return inv


def kernel(
    tok, gain, index, weight,
    gram_out, panel_out, proj_out,
    cols, rows, panel, gram, ext, inverse, white, part, landed,
    flipped, squares, masked, sums, trace_own, trace_t, trace_s, trace_sum,
    sq_send, sq_recv, rs_send, rs_recv, ag_send, ag_recv, tt_send, tt_recv, ts_send, ts_recv,
    p_send, p_recv, c_send, c_recv, r_send, r_recv, x_send, x_recv, x_local,
    f_send, f_recv, out_sem, wh_sem,
):
    s, t = lax.axis_index("seq"), lax.axis_index("tensor")
    i, core = s // 2, s % 2
    y, xl = i // 2, i % 2
    z, xh = t // 2, t % 2
    own = i == t
    start = index[0] * PANEL

    def seq_peer(k):
        return (k, t)

    def tensor_peer(k):
        return (s, k)

    value = tok[...].astype(F32)
    part_sq = jnp.zeros((128, 128), F32)
    for b in range(16):
        piece = value[:, b * 128 : (b + 1) * 128]
        part_sq = part_sq + piece * piece
    tile = lax.dot_general(
        jnp.ones((8, 128), F32), part_sq, (((1,), (1,)), ((), ())),
        precision=lax.Precision.HIGHEST, preferred_element_type=F32,
    )
    squares[0] = tile

    barrier = pltpu.get_barrier_semaphore()
    for d in range(1, 16):
        pl.semaphore_signal(barrier, inc=1, device_id=seq_peer((s + d) % 16), device_id_type=MESH)
    for d in range(1, 8):
        pl.semaphore_signal(barrier, inc=1, device_id=tensor_peer((t + d) % 8), device_id_type=MESH)

    @pl.when(jnp.logical_not(own))
    def _():
        for c in range(2):
            pl.semaphore_signal(barrier, inc=1, device_id=(2 * t + c, i), device_id_type=MESH)

    pl.semaphore_wait(barrier, jnp.where(own, 22, 24))

    def remote(src, dst, send, recv, device):
        return pltpu.make_async_remote_copy(
            src_ref=src, dst_ref=dst, send_sem=send, recv_sem=recv, device_id=device, device_id_type=MESH
        )

    def exchange(count, src, dst, send, recv, peer):
        copies = [remote(src(d), dst(d), send.at[d], recv.at[d], peer(d)) for d in range(1, count)]
        for copy in copies:
            copy.start()
        return copies

    sq = exchange(8, lambda d: squares.at[0], lambda d: squares.at[d], sq_send, sq_recv, lambda d: tensor_peer((t + d) % 8))
    for copy in sq:
        copy.wait_recv()
    total = squares[0]
    for d in range(1, 8):
        total = total + squares[d]
    scale = lax.rsqrt(total / D + EPSILON)
    scale = jnp.transpose(jnp.broadcast_to(scale[0:1, :], (128, 128)))

    own_rows = pl.ds(pl.multiple_of(core * 128, 128), 128)
    quarter = index[0] % 4
    chosen = [jnp.zeros((128, 128), F32) for _ in range(4)]
    trace = jnp.zeros((128, 128), F32)
    for b in range(16):
        lanes = slice(b * 128, (b + 1) * 128)
        scaled = tok[:, lanes].astype(F32) * scale * gain[:, lanes]
        rounded = scaled.astype(BF16)
        cols[i, own_rows, lanes] = rounded
        wide = rounded.astype(F32)
        trace = trace + wide * wide
        chosen[b % 4] = chosen[b % 4] + jnp.where(quarter == b // 4, wide, 0.0)
        flipped[lanes, :] = (jnp.transpose(wide) * (1.0 / TOKENS)).astype(BF16)
    mine = jnp.where(index[0] // 4 == t, 1.0, 0.0)
    for b in range(4):
        masked[:, b * 128 : (b + 1) * 128] = (chosen[b] * mine).astype(BF16)
    trace_own[...] = jnp.sum(trace.reshape(16, 8, 128), axis=0)

    def piece_rows(k):
        return pl.ds(pl.multiple_of(k * 16, 16), 16)

    rs = exchange(
        8, lambda d: masked.at[piece_rows((t + d) % 8)], lambda d: sums.at[d], rs_send, rs_recv, lambda d: tensor_peer((t + d) % 8)
    )
    tt = exchange(8, lambda d: trace_own, lambda d: trace_t.at[d], tt_send, tt_recv, lambda d: tensor_peer((t + d) % 8))

    def flip_src(c):
        return flipped.at[pl.ds(c * 1024, 1024)]

    def flip_dst(c):
        return rows.at[i, :, pl.ds(pl.multiple_of(c * 128, 128), 128)]

    @pl.when(jnp.logical_not(own))
    def _():
        for c in range(2):
            remote(flip_src(c), flip_dst(core), x_send.at[c], x_recv.at[core], (2 * t + c, i)).start()

    own_half = pl.ds(pl.multiple_of(core * 1024, 1024), 1024)
    other_half = pl.ds(pl.multiple_of((1 - core) * 1024, 1024), 1024)

    @pl.when(own)
    def _():
        remote(flipped.at[other_half], flip_dst(core), x_send.at[0], x_recv.at[core], seq_peer(s + 1 - 2 * core)).start()
        pltpu.make_async_copy(flipped.at[own_half], flip_dst(core), x_local).start()

    for copy in rs:
        copy.wait_recv()
    total = masked[piece_rows(t), :].astype(F32)
    for d in range(1, 8):
        total = total + sums[d].astype(F32)

    def panel_piece(k):
        return panel.at[i, pl.ds(pl.multiple_of(core * 128 + k * 16, 16), 16), :]

    panel[i, pl.ds(pl.multiple_of(core * 128 + t * 16, 16), 16), :] = total.astype(BF16)
    ag = [
        remote(panel_piece(t), panel_piece(t), ag_send.at[d], ag_recv.at[d], tensor_peer((t + d) % 8)) for d in range(1, 8)
    ]
    for copy in ag:
        copy.start()
    for copy in tt:
        copy.wait_recv()
    total = trace_own[...]
    for d in range(1, 8):
        total = total + trace_t[d]
    trace_sum[...] = total
    ts = exchange(16, lambda d: trace_sum, lambda d: trace_s.at[d], ts_send, ts_recv, lambda d: seq_peer((s + d) % 16))

    class Ring:
        def __init__(self, slot, send, recv, partner, up, down, sibling):
            self.slot, self.send, self.recv = slot, send, recv
            self.peers = {"X": partner, "P": up, "M": down, "S": sibling}
            self.sent = []

        ITEMS = ("B", "A-", "A+", "B-", "B+", "A--", "B++", "SA", "SB", "SA-", "SA+", "SB-", "SB+", "SA--", "SB++")
        AT = {"A": (0, 0), "B": (0, 1), "A-": (-1, 0), "A+": (1, 0), "B-": (-1, 1), "B+": (1, 1), "A--": (-2, 0), "B++": (2, 1)}

        def copy(self, item, peer, lands):
            k = self.ITEMS.index(lands)
            ref = self.slot(*self.AT[item])
            return remote(ref, ref, self.send.at[k], self.recv.at[k], self.peers[peer])

        def go(self, item, *targets):
            for peer, lands in targets:
                self.copy(item, peer, lands).start()
                self.sent.append((item, peer, lands))
            if self.peers["S"] is not None:
                self.copy(item, "S", "S" + item).start()
                self.sent.append((item, "S", "S" + item))

        def wait(self, item):
            k = self.ITEMS.index(item)
            ref = self.slot(*self.AT[item], flip=False) if item[0] != "S" else self.slot(*self.AT[item[1:]], flip=True)
            remote(ref, ref, self.send.at[k], self.recv.at[k], self.peers["P"]).wait_recv()

        def step0(self):
            self.go("A", ("P", "A-"), ("M", "A+"), ("X", "B"))

        def step1(self):
            self.wait("B")
            self.go("B", ("P", "B-"), ("M", "B+"))

        def step2(self):
            self.wait("A-")
            self.go("A-", ("P", "A--"))
            self.wait("A+")
            self.go("A+")

        def step3(self):
            self.wait("B+")
            self.go("B+", ("M", "B++"))
            self.wait("B-")
            self.go("B-")

        def step4(self):
            self.wait("A--")
            self.go("A--")
            self.wait("B++")
            self.go("B++")

        def siblings(self, *items):
            for item in items:
                self.wait("S" + item)

        def drain(self):
            for sent in self.sent:
                self.copy(*sent).wait_send()

    def half_slot(buffer):
        def slot(dy, dx, flip=False):
            chunk = ((y + dy + 4) % 4) * 2 + (xl + dx) % 2
            half = (1 - core) if flip else core
            return buffer.at[chunk, pl.ds(pl.multiple_of(half * 128, 128), 128), :]
        return slot

    def row_slot(dz, dx, flip=False):
        return rows.at[((z + dz + 4) % 4) * 2 + (xh + dx) % 2]

    seq_ring = (seq_peer(s + 2 - 4 * xl), seq_peer((s + 4) % 16), seq_peer((s + 12) % 16), seq_peer(s + 1 - 2 * core))
    c_ring = Ring(half_slot(cols), c_send, c_recv, *seq_ring)
    p_ring = Ring(half_slot(panel), p_send, p_recv, *seq_ring)
    r_ring = Ring(row_slot, r_send, r_recv, tensor_peer(t + 1 - 2 * xh), tensor_peer((t + 2) % 8), tensor_peer((t + 6) % 8), None)

    for copy in (
        remote(panel_piece((t + 8 - d) % 8), panel_piece((t + 8 - d) % 8), ag_send.at[d], ag_recv.at[d], tensor_peer((t + d) % 8))
        for d in range(1, 8)
    ):
        copy.wait_recv()
    p_ring.step0()
    c_ring.step0()
    p_ring.step1()

    def flip_land(c):
        return rows.at[t, :, pl.ds(c * 128, 128)]

    for c in range(2):
        @pl.when(jnp.logical_not(jnp.logical_and(own, core == c)))
        def _():
            remote(flip_land(c), flip_land(c), x_send.at[0], x_recv.at[c], seq_peer(s + 1 - 2 * core)).wait_recv()

    @pl.when(own)
    def _():
        pltpu.make_async_copy(flipped.at[own_half], flip_dst(core), x_local).wait()

    r_ring.step0()
    p_ring.step2()
    p_ring.step3()
    p_ring.step4()
    c_ring.step1()
    p_ring.siblings("A", "B", "A-", "A+", "B-", "B+", "A--", "B++")
    r_ring.step1()

    for copy in ts:
        copy.wait_recv()
    total = trace_sum[...]
    for d in range(1, 16):
        total = total + trace_s[d]
    shift = DAMPING * (jnp.sum(total) / TOKENS) / D

    def fill(b, _):
        at = pl.ds(pl.multiple_of(b * 128, 128), 128)
        block = jnp.zeros((128, 512), F32)
        for k in range(8):
            block = block + dot(panel[k, :, at], panel[k], ((0,), (0,)))
        eye = (
            b * 128 + lax.broadcasted_iota(jnp.int32, (128, 512), 0)
            == lax.broadcasted_iota(jnp.int32, (128, 512), 1)
        )
        ext[at, 0:512] = block * (1.0 / TOKENS) + jnp.where(eye, shift, 0.0)
        ext[at, 512:1024] = jnp.where(eye, 1.0, 0.0)
        return 0

    lax.fori_loop(0, 4, fill, 0)

    def factor(b, _):
        base = b * 128
        at = pl.ds(pl.multiple_of(base, 128), 128)
        tiles = [ext[pl.ds(pl.multiple_of(base + 8 * g, 8), 8), at] for g in range(16)]
        inv = jnp.concatenate(inverse_factor(tiles), axis=0)
        upper = dot_split(inv, ext[at, :], ((1,), (0,)))
        inverse[at, :] = upper[:, 512:1024]
        for k in range(4):
            lanes = slice(k * 128, (k + 1) * 128)
            ext[lanes, :] = ext[lanes, :] - dot_split(upper[:, lanes], upper, ((0,), (0,)))

        return 0

    def gram_chunks(late):
        def body(k, _):
            ky = k // 2
            is_late = jnp.logical_or(ky == (y + 2) % 4, ky == jnp.where(y == z, (y + 3) % 4, (z + 2) % 4))
            @pl.when(is_late == late)
            def _():
                @pl.loop(0, 4)
                def _(m):
                    band = pl.ds(pl.multiple_of(m * 256, 256), 256)
                    for n in range(4):
                        lanes = slice(n * 512, (n + 1) * 512)
                        gram[band, lanes] += dot(rows[k, band, :], cols[k, :, lanes], ((1,), (0,)))
            return 0

        lax.fori_loop(0, 8, body, 0)

    @pl.loop(0, 8)
    def _(m):
        gram[pl.ds(pl.multiple_of(m * 128, 128), 128), :] = jnp.zeros((128, 2048), F32)

    def factor_and_forward(b, _):
        factor(b, 0)

        @pl.when(b == 0)
        def _():
            c_ring.step2()
            r_ring.step2()

        @pl.when(b == 2)
        def _():
            c_ring.step3()
            r_ring.step3()

        return 0

    lax.fori_loop(0, 4, factor_and_forward, 0)
    c_ring.siblings("A", "B", "A-", "A+", "B-", "B+")
    gram_chunks(False)
    r_ring.wait("A--")
    r_ring.wait("B++")

    @pl.loop(0, 8)
    def _(m):
        band = pl.ds(pl.multiple_of(m * 128, 128), 128)
        block = jnp.zeros((128, 512), F32)
        for k in range(8):
            block = block + dot(rows[k, band, :], panel[k], ((1,), (0,)))
        at = s * 1024 + m * 128 - start
        eye = at + lax.broadcasted_iota(jnp.int32, (128, 512), 0) == lax.broadcasted_iota(jnp.int32, (128, 512), 1)
        block = block + jnp.where(eye, shift, 0.0)
        white[band, :] = dot_split(block, inverse[...], ((1,), (1,))).astype(BF16)

    white_copy = pltpu.make_async_copy(white, panel_out, wh_sem)
    white_copy.start()
    for k in range(4):
        lanes = slice(k * 128, (k + 1) * 128)
        part[lanes, :] = dot(white[:, lanes], weight[...], ((0,), (1,)))

    def part_rows(k):
        return part.at[pl.ds(pl.multiple_of(k * 32, 32), 32)]

    fs = exchange(
        16, lambda d: part_rows((s + d) % 16), lambda d: landed.at[d], f_send, f_recv, lambda d: seq_peer((s + d) % 16)
    )
    c_ring.step4()
    c_ring.siblings("A--", "B++")
    gram_chunks(True)

    @pl.when(own)
    def _():
        @pl.loop(0, 8)
        def _(m):
            band = pl.ds(pl.multiple_of(m * 128, 128), 128)
            at = pl.ds(pl.multiple_of(core * 1024 + m * 128, 128), 128)
            eye = lax.broadcasted_iota(jnp.int32, (128, 128), 0) == lax.broadcasted_iota(jnp.int32, (128, 128), 1)
            gram[band, at] += jnp.where(eye, shift, 0.0)

    gram_copy = pltpu.make_async_copy(gram, gram_out, out_sem)
    gram_copy.start()
    for copy in fs:
        copy.wait_recv()
    total = part[pl.ds(pl.multiple_of(s * 32, 32), 32), :]
    for d in range(1, 16):
        total = total + landed[d]
    total = jnp.concatenate([total, jnp.zeros((96, 256), F32)], axis=0)
    proj_out[...] = jnp.transpose(total)[:, 0:32]

    for copies in (sq, rs, tt, ag, ts, fs):
        for copy in copies:
            copy.wait_send()
    for ring in (p_ring, c_ring, r_ring):
        ring.drain()
    remote(flipped.at[own_half], flip_dst(core), x_send.at[0], x_recv.at[0], seq_peer(s + 1 - 2 * core)).wait_send()

    @pl.when(jnp.logical_not(own))
    def _():
        remote(flipped.at[own_half], flip_dst(core), x_send.at[1], x_recv.at[0], seq_peer(s + 1 - 2 * core)).wait_send()

    white_copy.wait()
    gram_copy.wait()


def on_device(tokens, norm_gain, projection_weight, panel_index):
    vmem = pl.BlockSpec(memory_space=pltpu.VMEM)
    anywhere = pl.BlockSpec(memory_space=pl.ANY)
    dma = pltpu.SemaphoreType.DMA
    return pl.pallas_call(
        kernel,
        out_shape=(
            jax.ShapeDtypeStruct((1024, 2048), F32),
            jax.ShapeDtypeStruct((1024, 512), BF16),
            jax.ShapeDtypeStruct((256, 32), F32),
        ),
        in_specs=[vmem, vmem, pl.BlockSpec(memory_space=pltpu.SMEM), vmem],
        out_specs=(anywhere, anywhere, vmem),
        scratch_shapes=[
            pltpu.VMEM((8, 256, 2048), BF16),
            pltpu.VMEM((8, 1024, 256), BF16),
            pltpu.VMEM((8, 256, 512), BF16),
            pltpu.VMEM((1024, 2048), F32),
            pltpu.VMEM((512, 1024), F32),
            pltpu.VMEM((512, 512), F32),
            pltpu.VMEM((1024, 512), BF16),
            pltpu.VMEM((512, 256), F32),
            pltpu.VMEM((16, 32, 256), F32),
            pltpu.VMEM((2048, 128), BF16),
            pltpu.VMEM((8, 8, 128), F32),
            pltpu.VMEM((128, 512), BF16),
            pltpu.VMEM((8, 16, 512), BF16),
            pltpu.VMEM((8, 128), F32),
            pltpu.VMEM((8, 8, 128), F32),
            pltpu.VMEM((16, 8, 128), F32),
            pltpu.VMEM((8, 128), F32),
            dma((8,)), dma((8,)), dma((8,)), dma((8,)), dma((8,)), dma((8,)), dma((8,)), dma((8,)), dma((16,)), dma((16,)),
            dma((15,)), dma((15,)), dma((15,)), dma((15,)), dma((15,)), dma((15,)), dma((2,)), dma((2,)), dma,
            dma((16,)), dma((16,)), dma, dma,
        ],
        compiler_params=pltpu.CompilerParams(
            collective_id=0, has_side_effects=True, vmem_limit_bytes=50 * 1024 * 1024
        ),
        cost_estimate=pl.CostEstimate(flops=12_000_000_000, bytes_accessed=20_000_000, transcendentals=0),
        name="whiten",
    )(tokens, norm_gain[None, :], panel_index, projection_weight)


def solution(mesh):
    placed = (P("seq", "tensor"), P("tensor"), P("tensor", "seq"), P())
    return jax.shard_map(
        on_device,
        mesh=mesh,
        in_specs=placed,
        out_specs=(P("seq", "tensor"), P("seq", None), P("tensor", "seq")),
        check_vma=False,
    )
```

```python
import functools

import jax
import jax.numpy as jnp
from jax import lax
from jax.experimental import pallas as pl
from jax.experimental.pallas import tpu as pltpu
from jax.sharding import PartitionSpec as P

D = 16384
PANEL = 512
TOKENS = 2048
EPSILON = 1e-05
DAMPING = 0.1
F32 = jnp.float32
BF16 = jnp.bfloat16
MESH = pl.DeviceIdType.MESH


def halves(a):
    high = a.astype(BF16)
    return high, (a - high.astype(F32)).astype(BF16)


def dot(a, b, dims):
    return lax.dot_general(a, b, (dims, ((), ())), preferred_element_type=F32)


def dot_split(a, b, dims):
    ah, al = halves(a)
    bh, bl = halves(b)
    return dot(ah, bh, dims) + (dot(ah, bl, dims) + dot(al, bh, dims))


def row_of(tile, r):
    return jnp.broadcast_to(tile[r : r + 1, :], (8, 128))


def column_of(tile, k):
    return jnp.broadcast_to(tile[:, k : k + 1], (8, 128))


def inverse_factor(a):
    sub = lax.broadcasted_iota(jnp.int32, (8, 128), 0)
    lane = lax.broadcasted_iota(jnp.int32, (8, 128), 1)
    inv = [jnp.where(sub + 8 * g == lane, 1.0, 0.0).astype(F32) for g in range(16)]
    for g in range(16):
        cols = [{k: column_of(a[k], 8 * g + c) for k in range(g, 16)} for c in range(8)]
        for c in range(8):
            r = lax.rsqrt(row_of(cols[c][g], c))
            m = {k: cols[c][k] * r for k in range(g, 16)}
            for c2 in range(c + 1, 8):
                f = row_of(cols[c2][g], c) * r
                for k in range(g, 16):
                    cols[c2][k] = cols[c2][k] - m[k] * f
            u = row_of(a[g], c) * r
            z = row_of(inv[g], c) * r
            m[g] = jnp.where(sub > c, m[g], 0.0)
            for k in range(g, 16):
                a[k] = a[k] - m[k] * u
                inv[k] = inv[k] - m[k] * z
            inv[g] = jnp.where(sub == c, z, inv[g])
    return inv


def kernel(
    tok_hbm, gain_hbm, index, weight_hbm,
    gram, white, proj_out,
    tok, gain, weight, cols, rows, panel, ext, inverse, part, landed,
    flipped, squares, masked, sums, gain_own, gain_t, scales, trace_own, trace_t, trace_s, trace_sum,
    in_sem, sq_send, sq_recv, rs_send, rs_recv, gt_send, gt_recv, ag_send, ag_recv, tt_send, tt_recv, ts_send, ts_recv,
    p_send, p_recv, c_send, c_recv, r_send, r_recv, x_send, x_recv, x_local, y_send, y_recv, relay, gain_far, scale_lanes, right, f_send, f_recv,
):
    s, t = lax.axis_index("seq"), lax.axis_index("tensor")
    i, core = s // 2, s % 2
    y, xl = i // 2, i % 2
    z, xh = t // 2, t % 2
    start = index[0] * PANEL
    first = ((z + 4 - y) % 4) * 2 + xh
    mirror = 2 * z + xl
    shifted = ((z + y) % 4) * 2 + xh
    own = jnp.logical_and(first == i, mirror == t)

    def seq_peer(k):
        return (k, t)

    def tensor_peer(k):
        return (s, k)

    fetch = [
        pltpu.make_async_copy(tok_hbm, tok, in_sem.at[0]),
        pltpu.make_async_copy(gain_hbm, gain, in_sem.at[1]),
        pltpu.make_async_copy(weight_hbm, weight, in_sem.at[2]),
    ]
    for copy in fetch:
        copy.start()

    barrier = pltpu.get_barrier_semaphore()
    for d in range(1, 16):
        pl.semaphore_signal(barrier, inc=1, device_id=seq_peer((s + d) % 16), device_id_type=MESH)
    for d in range(1, 8):
        pl.semaphore_signal(barrier, inc=1, device_id=tensor_peer((t + d) % 8), device_id_type=MESH)

    @pl.when(xl != xh)
    def _():
        for c in range(2):
            pl.semaphore_signal(barrier, inc=1, device_id=(2 * first + c, mirror), device_id_type=MESH)

    fetch[0].wait()
    fetch[1].wait()
    quarter = index[0] % 4
    mine = index[0] // 4 == t
    chosen = [jnp.zeros((128, 128), F32) for _ in range(4)]
    part_sq = jnp.zeros((128, 128), F32)
    for b in range(16):
        piece = tok[:, b * 128 : (b + 1) * 128].astype(F32)
        part_sq = part_sq + piece * piece
        flipped[b * 128 : (b + 1) * 128, :] = jnp.transpose(piece).astype(BF16)
        taken = jnp.logical_and(mine, quarter == b // 4)
        chosen[b % 4] = chosen[b % 4] + jnp.where(taken, piece, 0.0)
    for b in range(4):
        masked[:, b * 128 : (b + 1) * 128] = chosen[b].astype(BF16)
    taken = jnp.zeros((1, 512), F32)
    for b in range(4):
        taken = taken + jnp.where(jnp.logical_and(mine, quarter == b), gain[:, b * 512 : (b + 1) * 512], 0.0)
    gain_own[...] = jnp.broadcast_to(taken, (8, 512))
    squares[0] = lax.dot_general(
        jnp.ones((8, 128), F32), part_sq, (((1,), (1,)), ((), ())),
        precision=lax.Precision.HIGHEST, preferred_element_type=F32,
    )

    pl.semaphore_wait(barrier, jnp.where(xl == xh, 22, 24))

    def remote(src, dst, send, recv, device):
        return pltpu.make_async_remote_copy(
            src_ref=src, dst_ref=dst, send_sem=send, recv_sem=recv, device_id=device, device_id_type=MESH
        )

    def exchange(count, src, dst, send, recv, peer):
        copies = [remote(src(d), dst(d), send.at[d], recv.at[d], peer(d)) for d in range(1, count)]
        for copy in copies:
            copy.start()
        return copies

    def piece_rows(k):
        return pl.ds(pl.multiple_of(k * 16, 16), 16)

    def across(d):
        return tensor_peer((t + d) % 8)

    def along(d):
        return seq_peer((s + d) % 16)

    sq = exchange(8, lambda d: squares.at[0], lambda d: squares.at[d], sq_send, sq_recv, across)
    rs = exchange(8, lambda d: masked.at[piece_rows((t + d) % 8)], lambda d: sums.at[d], rs_send, rs_recv, across)
    gt = exchange(8, lambda d: gain_own, lambda d: gain_t.at[d], gt_send, gt_recv, across)
    def quarter_of(src, c, q):
        return src.at[pl.ds(c * 1024 + q * 512, 512)]

    def landing(chunk, c, q):
        return rows.at[chunk, c, pl.ds(q * 512, 512)]

    def into_rows(c, q, src):
        sem = 2 * q + c
        return remote(
            quarter_of(src, c, q), landing(i, core, q), x_send.at[sem], x_recv.at[2 * q + core], (2 * first + c, mirror)
        )

    def to_shifted(c, q):
        sem = 2 * q + c
        return remote(quarter_of(flipped, c, q), quarter_of(relay, c, q), y_send.at[sem], y_recv.at[sem], tensor_peer(shifted))

    def gain_to_shifted():
        return remote(gain, gain_far, y_send.at[4], y_recv.at[4], tensor_peer(shifted))

    def shift_start(q):
        @pl.when(y != 0)
        def _():
            if q == 0:
                gain_to_shifted().start()
            else:
                for c in range(2):
                    to_shifted(c, 0).wait_send()
            for c in range(2):
                to_shifted(c, q).start()

    def to_mirror(src, gains, q):
        for c in range(2):
            @pl.loop(0, 4)
            def _(b):
                at = pl.ds(pl.multiple_of(c * 1024 + q * 512 + b * 128, 128), 128)
                by_row = jnp.transpose(jnp.broadcast_to(gains[:, at], (128, 128)))
                by_lane = jnp.broadcast_to(scale_lanes[0:1, :], (128, 128))
                src[at, :] = (src[at, :].astype(F32) * by_lane * by_row * (1.0 / TOKENS)).astype(BF16)

            keeps = jnp.logical_and(own, core == c)

            @pl.when(keeps)
            def _():
                pltpu.make_async_copy(quarter_of(src, c, q), landing(i, core, q), x_local.at[q]).start()

            @pl.when(jnp.logical_not(keeps))
            def _():
                into_rows(c, q, src).start()

    def relay_on(q):
        @pl.when(y == 0)
        def _():
            to_mirror(flipped, gain, q)

        @pl.when(y != 0)
        def _():
            if q == 0:
                gain_to_shifted().wait_recv()
            for c in range(2):
                to_shifted(c, q).wait_recv()
            to_mirror(relay, gain_far, q)

    def landed_rows(q):
        for c in range(2):
            @pl.when(jnp.logical_not(jnp.logical_and(own, core == c)))
            def _():
                there = landing(first, c, q)
                remote(there, there, x_send.at[0], x_recv.at[2 * q + c], seq_peer(s + 1 - 2 * core)).wait_recv()

        @pl.when(own)
        def _():
            pltpu.make_async_copy(quarter_of(flipped, 0, q), landing(i, core, q), x_local.at[q]).wait()

    shift_start(0)
    for copy in sq:
        copy.wait_recv()
    total = squares[0]
    for d in range(1, 8):
        total = total + squares[d]
    scale = lax.rsqrt(total / D + EPSILON)
    scale_lanes[...] = scale
    scale = jnp.transpose(jnp.broadcast_to(scale[0:1, :], (128, 128)))
    scales[...] = scale
    shift_start(1)

    for copy in rs + gt:
        copy.wait_recv()
    total = masked[piece_rows(t), :].astype(F32)
    total_gain = gain_own[0:1, :]
    for d in range(1, 8):
        total = total + sums[d].astype(F32)
        total_gain = total_gain + gain_t[d, 0:1, :]

    def panel_piece(k):
        return panel.at[i, pl.ds(pl.multiple_of(core * 128 + k * 16, 16), 16), :]

    piece_scale = scales[piece_rows(t), :]
    for b in range(4):
        lanes = slice(b * 128, (b + 1) * 128)
        panel[i, pl.ds(pl.multiple_of(core * 128 + t * 16, 16), 16), lanes] = (
            total[:, lanes] * piece_scale * total_gain[:, lanes]
        ).astype(BF16)
    ag = [remote(panel_piece(t), panel_piece(t), ag_send.at[d], ag_recv.at[d], across(d)) for d in range(1, 8)]
    for copy in ag:
        copy.start()

    relay_on(0)
    own_rows = pl.ds(pl.multiple_of(core * 128, 128), 128)
    trace = jnp.zeros((128, 128), F32)
    for b in range(16):
        lanes = slice(b * 128, (b + 1) * 128)
        scaled = tok[:, lanes].astype(F32) * scale * gain[:, lanes]
        rounded = scaled.astype(BF16)
        cols[i, own_rows, lanes] = rounded
        wide = rounded.astype(F32)
        trace = trace + wide * wide
    trace_own[...] = jnp.sum(trace.reshape(16, 8, 128), axis=0)
    tt = exchange(8, lambda d: trace_own, lambda d: trace_t.at[d], tt_send, tt_recv, across)

    class Ring:
        ITEMS = ("B", "A-", "A+", "B-", "B+", "A--", "B++", "C-", "C+", "C--")
        AT = {
            "A": (0, 0), "B": (0, 1), "A-": (-1, 0), "A+": (1, 0), "B-": (-1, 1), "B+": (1, 1), "A--": (-2, 0), "B++": (2, 1),
            "C-": (-1, 1), "C+": (1, 1), "C--": (2, 1),
        }

        def __init__(self, slot, send, recv, partner, up, down, sibling, split=None):
            self.slot, self.send, self.recv, self.split = slot, send, recv, split
            self.peers = {"X": partner, "P": up, "M": down, "S": sibling}
            self.sent = []

        def part(self, kind):
            if self.split is None:
                return None
            return {"A": None, "B": (0, self.split), "C": (self.split, 128)}[kind]

        def copy(self, item, peer, lands):
            k = (11 if lands[0] == "S" else 0) + (("A",) + self.ITEMS).index(lands.lstrip("S"))
            kind = lands.lstrip("S")[0]
            ref = self.slot(*self.AT[item], rows=None if lands.lstrip("S") == "B" else self.part(kind))
            return remote(ref, ref, self.send.at[k], self.recv.at[k], self.peers[peer])

        def go(self, item, *targets):
            if self.peers["S"] is not None:
                targets = targets + (("S", "S" + item),)
            for peer, lands in targets:
                self.copy(item, peer, lands).start()
                self.sent.append((item, peer, lands))

        def wait(self, item):
            k = (11 if item[0] == "S" else 0) + (("A",) + self.ITEMS).index(item.lstrip("S"))
            name = item.lstrip("S")
            ref = self.slot(*self.AT[name], flip=item[0] == "S", rows=None if name == "B" else self.part(name[0]))
            remote(ref, ref, self.send.at[k], self.recv.at[k], self.peers["P"]).wait_recv()

        def across(self, lands):
            return () if self.split is None else (("X", lands),)

        def step0(self):
            self.go("A", ("P", "A-"), ("M", "A+"), ("X", "B"))

        def step1(self):
            self.wait("B")
            self.go("B", ("P", "B-"), ("M", "B+"))

        def step2(self):
            self.wait("A-")
            self.go("A-", ("P", "A--"), *self.across("C-"))
            self.wait("A+")
            self.go("A+", *self.across("C+"))

        def step3(self):
            self.wait("B+")
            self.go("B+", ("M", "B++"))
            self.wait("B-")
            self.go("B-")
            if self.split is not None:
                self.wait("C-")
                self.go("C-")
                self.wait("C+")
                self.go("C+")

        def step4(self):
            self.wait("A--")
            self.go("A--", *self.across("C--"))
            self.wait("B++")
            self.go("B++")

        def step5(self):
            self.wait("C--")
            self.go("C--")

        def siblings(self, *items):
            for item in items:
                self.wait("S" + item)

        def drain(self):
            for sent in self.sent:
                self.copy(*sent).wait_send()

    def half_slot(buffer):
        def slot(dy, dx, flip=False, rows=None):
            low, high = rows or (0, 128)
            chunk = ((y + dy + 4) % 4) * 2 + (xl + dx) % 2
            half = (1 - core) if flip else core
            return buffer.at[chunk, pl.ds(pl.multiple_of(half * 128 + low, 16), high - low), :]
        return slot

    def row_slot(dz, dx, **_):
        return rows.at[((z + 8 + dz - y) % 4) * 2 + (xh + dx) % 2]

    def row_part(q):
        return lambda dz, dx, **_: row_slot(dz, dx).at[:, pl.ds(q * 512, 512)]

    seq_ring = (seq_peer(s + 2 - 4 * xl), seq_peer((s + 4) % 16), seq_peer((s + 12) % 16), seq_peer(s + 1 - 2 * core))
    c_ring = Ring(half_slot(cols), c_send, c_recv, *seq_ring, split=80)
    p_ring = Ring(half_slot(panel), p_send, p_recv, *seq_ring)
    z_ring = (tensor_peer(t + 1 - 2 * xh), tensor_peer((t + 2) % 8), tensor_peer((t + 6) % 8), None)
    r_ring = [Ring(row_part(q), r_send.at[q], r_recv.at[q], *z_ring) for q in range(2)]

    for d in range(1, 8):
        there = panel_piece((t + 8 - d) % 8)
        remote(there, there, ag_send.at[d], ag_recv.at[d], across(d)).wait_recv()
    p_ring.step0()

    for copy in tt:
        copy.wait_recv()
    total = trace_own[...]
    for d in range(1, 8):
        total = total + trace_t[d]
    trace_sum[...] = total
    ts = exchange(16, lambda d: trace_sum, lambda d: trace_s.at[d], ts_send, ts_recv, along)
    p_ring.step1()
    relay_on(1)
    p_ring.step2()
    p_ring.step3()
    c_ring.step0()
    landed_rows(0)
    r_ring[0].step0()
    p_ring.step4()
    p_ring.siblings("A", "B", "A-", "A+", "B-", "B+", "A--", "B++")

    for copy in ts:
        copy.wait_recv()
    total = trace_sum[...]
    for d in range(1, 16):
        total = total + trace_s[d]
    shift = DAMPING * (jnp.sum(total) / TOKENS) / D

    def fill(b, _):
        at = pl.ds(pl.multiple_of(b * 128, 128), 128)
        block = jnp.zeros((128, 512), F32)
        for k in range(8):
            block = block + dot(panel[k, :, at], panel[k], ((0,), (0,)))
        eye = (
            b * 128 + lax.broadcasted_iota(jnp.int32, (128, 512), 0)
            == lax.broadcasted_iota(jnp.int32, (128, 512), 1)
        )
        ext[at, 0:512] = block * (1.0 / TOKENS) + jnp.where(eye, shift, 0.0)
        ext[at, 512:1024] = jnp.where(eye, 1.0, 0.0)
        return 0

    lax.fori_loop(0, 4, fill, 0)
    landed_rows(1)
    r_ring[1].step0()
    c_ring.step1()

    far = (y + 2) % 4
    apart = (z + 8 - 2 * y) % 4
    early = [(far + jnp.where(apart >= 2, 1, 2)) % 4, (far + jnp.where(apart == 3, 2, 3)) % 4]
    late = [far, (far + jnp.where(apart == 0, 1, apart)) % 4]

    def row_band(k, band):
        return jnp.concatenate([rows[k, 0, band, :], rows[k, 1, band, :]], axis=1)

    def product(chunks, band, right_of):
        total = None
        for ky in chunks:
            for kx in range(2):
                k = ky * 2 + kx
                term = dot(row_band(k, band), right_of(k), ((1,), (0,)))
                total = term if total is None else total + term
        return total

    def gram_band(chunks, band):
        for n in range(4):
            lanes = slice(n * 512, (n + 1) * 512)
            yield lanes, product(chunks, band, lambda k: cols[k, :, lanes])

    def factor(b):
        base = b * 128
        at = pl.ds(pl.multiple_of(base, 128), 128)
        tiles = [ext[pl.ds(pl.multiple_of(base + 8 * g, 8), 8), at] for g in range(16)]
        inv = jnp.concatenate(inverse_factor(tiles), axis=0)
        upper = dot_split(inv, ext[at, :], ((1,), (0,)))
        inverse[at, :] = upper[:, 512:1024]
        for k in range(4):
            lanes = slice(k * 128, (k + 1) * 128)
            ext[lanes, :] = ext[lanes, :] - dot_split(upper[:, lanes], upper, ((0,), (0,)))

    def factor_and_forward(b, _):
        factor(b)

        @pl.when(b == 0)
        def _():
            r_ring[0].step1()
            c_ring.step2()
            r_ring[0].step2()

        @pl.when(b == 1)
        def _():
            r_ring[1].step1()
            c_ring.step3()
            r_ring[1].step2()

        @pl.when(b == 2)
        def _():
            r_ring[0].step3()
            r_ring[1].step3()
            c_ring.step4()

        @pl.when(b == 3)
        def _():
            c_ring.step5()

        return 0

    lax.fori_loop(0, 4, factor_and_forward, 0)
    c_ring.siblings("A", "B", "A-", "A+", "B-", "B+", "C-", "C+")

    @pl.loop(0, 8)
    def _(m):
        band = pl.ds(pl.multiple_of(m * 128, 128), 128)
        right[band, :] = product(early, band, lambda k: panel[k])
        for lanes, value in gram_band(early, band):
            gram[band, lanes] = value

    for ring in r_ring:
        ring.wait("A--")
        ring.wait("B++")

    @pl.loop(0, 8)
    def _(m):
        band = pl.ds(pl.multiple_of(m * 128, 128), 128)
        at = s * 1024 + m * 128 - start
        eye = at + lax.broadcasted_iota(jnp.int32, (128, 512), 0) == lax.broadcasted_iota(jnp.int32, (128, 512), 1)
        block = right[band, :] + product(late, band, lambda k: panel[k]) + jnp.where(eye, shift, 0.0)
        white[band, :] = dot_split(block, inverse[...], ((1,), (1,))).astype(BF16)

    fetch[2].wait()
    for k in range(4):
        lanes = slice(k * 128, (k + 1) * 128)
        part[lanes, :] = dot(white[:, lanes], weight[...], ((0,), (1,)))

    def part_rows(k):
        return part.at[pl.ds(pl.multiple_of(k * 32, 32), 32)]

    fs = exchange(16, lambda d: part_rows((s + d) % 16), lambda d: landed.at[d], f_send, f_recv, along)
    c_ring.siblings("A--", "B++", "C--")

    @pl.loop(0, 8)
    def _(m):
        band = pl.ds(pl.multiple_of(m * 128, 128), 128)
        for lanes, value in gram_band(late, band):
            gram[band, lanes] = gram[band, lanes] + value

    @pl.when(i == t)
    def _():
        @pl.loop(0, 8)
        def _(m):
            band = pl.ds(pl.multiple_of(m * 128, 128), 128)
            at = pl.ds(pl.multiple_of(core * 1024 + m * 128, 128), 128)
            eye = lax.broadcasted_iota(jnp.int32, (128, 128), 0) == lax.broadcasted_iota(jnp.int32, (128, 128), 1)
            gram[band, at] += jnp.where(eye, shift, 0.0)

    for copy in fs:
        copy.wait_recv()
    total = part[pl.ds(pl.multiple_of(s * 32, 32), 32), :]
    for d in range(1, 16):
        total = total + landed[d]
    proj_out[...] = total

    for copies in (sq, rs, gt, tt, ag, ts, fs):
        for copy in copies:
            copy.wait_send()
    for ring in (p_ring, c_ring, *r_ring):
        ring.drain()
    for c in range(2):
        @pl.when(jnp.logical_not(jnp.logical_and(own, core == c)))
        def _():
            for q in range(2):
                into_rows(c, q, flipped).wait_send()

        @pl.when(y != 0)
        def _():
            to_shifted(c, 1).wait_send()

    @pl.when(y != 0)
    def _():
        gain_to_shifted().wait_send()


def on_device(tokens, norm_gain, projection_weight, panel_index):
    vmem = pl.BlockSpec(memory_space=pltpu.VMEM)
    hbm = pl.BlockSpec(memory_space=pltpu.HBM)
    dma = pltpu.SemaphoreType.DMA
    gram, white, projected = pl.pallas_call(
        kernel,
        out_shape=(
            jax.ShapeDtypeStruct((1024, 2048), F32),
            jax.ShapeDtypeStruct((1024, 512), BF16),
            jax.ShapeDtypeStruct((32, 256), F32),
        ),
        in_specs=[hbm, hbm, pl.BlockSpec(memory_space=pltpu.SMEM), hbm],
        out_specs=(vmem, vmem, vmem),
        scratch_shapes=[
            pltpu.VMEM((128, 2048), BF16),
            pltpu.VMEM((1, 2048), F32),
            pltpu.VMEM((256, 1024), BF16),
            pltpu.VMEM((8, 256, 2048), BF16),
            pltpu.VMEM((8, 2, 1024, 128), BF16),
            pltpu.VMEM((8, 256, 512), BF16),
            pltpu.VMEM((512, 1024), F32),
            pltpu.VMEM((512, 512), F32),
            pltpu.VMEM((512, 256), F32),
            pltpu.VMEM((16, 32, 256), F32),
            pltpu.VMEM((2048, 128), BF16),
            pltpu.VMEM((8, 8, 128), F32),
            pltpu.VMEM((128, 512), BF16),
            pltpu.VMEM((8, 16, 512), BF16),
            pltpu.VMEM((8, 512), F32),
            pltpu.VMEM((8, 8, 512), F32),
            pltpu.VMEM((128, 128), F32),
            pltpu.VMEM((8, 128), F32),
            pltpu.VMEM((8, 8, 128), F32),
            pltpu.VMEM((16, 8, 128), F32),
            pltpu.VMEM((8, 128), F32),
            dma((3,)),
            dma((8,)), dma((8,)), dma((8,)), dma((8,)), dma((8,)), dma((8,)),
            dma((8,)), dma((8,)), dma((8,)), dma((8,)), dma((16,)), dma((16,)),
            dma((22,)), dma((22,)), dma((22,)), dma((22,)), dma((2, 22)), dma((2, 22)), dma((4,)), dma((4,)), dma((2,)), dma((5,)), dma((5,)),
            pltpu.VMEM((2048, 128), BF16), pltpu.VMEM((1, 2048), F32), pltpu.VMEM((8, 128), F32),
            pltpu.VMEM((1024, 512), F32), dma((16,)), dma((16,)),
        ],
        compiler_params=pltpu.CompilerParams(
            collective_id=0, has_side_effects=True, vmem_limit_bytes=36 * 1024 * 1024
        ),
        cost_estimate=pl.CostEstimate(flops=12_000_000_000, bytes_accessed=20_000_000, transcendentals=0),
        name="whiten",
    )(tokens, norm_gain[None, :], panel_index, projection_weight)
    return gram, white, projected.T


def solution(mesh):
    placed = (P("seq", "tensor"), P("tensor"), P("tensor", "seq"), P())
    return jax.shard_map(
        on_device,
        mesh=mesh,
        in_specs=placed,
        out_specs=(P("seq", "tensor"), P("seq", None), P("tensor", "seq")),
        check_vma=False,
    )
```

```python
import functools

import jax
import jax.numpy as jnp
from jax import lax
from jax.experimental import pallas as pl
from jax.experimental.pallas import tpu as pltpu
from jax.sharding import PartitionSpec as P

D = 16384
PANEL = 512
TOKENS = 2048
EPSILON = 1e-05
DAMPING = 0.1
BAND = 512
F32 = jnp.float32
BF16 = jnp.bfloat16
MESH = pl.DeviceIdType.MESH


def halves(a):
    high = a.astype(BF16)
    return high, (a - high.astype(F32)).astype(BF16)


def dot(a, b, dims):
    return lax.dot_general(a, b, (dims, ((), ())), preferred_element_type=F32)


def dot_split(a, b, dims):
    ah, al = halves(a)
    bh, bl = halves(b)
    return dot(ah, bh, dims) + (dot(ah, bl, dims) + dot(al, bh, dims))


def row_of(tile, r):
    return jnp.broadcast_to(tile[r : r + 1, :], (8, 128))


def column_of(tile, k):
    return jnp.broadcast_to(tile[:, k : k + 1], (8, 128))


def inverse_factor(a):
    sub = lax.broadcasted_iota(jnp.int32, (8, 128), 0)
    lane = lax.broadcasted_iota(jnp.int32, (8, 128), 1)
    inv = [jnp.where(sub + 8 * g == lane, 1.0, 0.0).astype(F32) for g in range(16)]
    for g in range(16):
        cols = [{k: column_of(a[k], 8 * g + c) for k in range(g, 16)} for c in range(8)]
        for c in range(8):
            r = lax.rsqrt(row_of(cols[c][g], c))
            m = {k: cols[c][k] * r for k in range(g, 16)}
            for c2 in range(c + 1, 8):
                f = row_of(cols[c2][g], c) * r
                for k in range(g, 16):
                    cols[c2][k] = cols[c2][k] - m[k] * f
            u = row_of(a[g], c) * r
            z = row_of(inv[g], c) * r
            m[g] = jnp.where(sub > c, m[g], 0.0)
            for k in range(g, 16):
                a[k] = a[k] - m[k] * u
                inv[k] = inv[k] - m[k] * z
            inv[g] = jnp.where(sub == c, z, inv[g])
    return inv


def kernel(
    tok_hbm, gain_hbm, index, weight_hbm,
    gram, white, proj_out,
    tok, gain, weight, cols, rows, panel, ext, inverse, part, landed,
    flipped, squares, masked, sums, gain_own, gain_t, scales, trace_own, trace_t, trace_s, trace_sum,
    in_sem, sq_send, sq_recv, rs_send, rs_recv, gt_send, gt_recv, ag_send, ag_recv, tt_send, tt_recv, ts_send, ts_recv,
    p_send, p_recv, c_send, c_recv, r_send, r_recv, x_send, x_recv, x_local, y_send, y_recv, relay, gain_far, scale_lanes, right, above, f_send, f_recv,
):
    s, t = lax.axis_index("seq"), lax.axis_index("tensor")
    i, core = s // 2, s % 2
    y, xl = i // 2, i % 2
    z, xh = t // 2, t % 2
    start = index[0] * PANEL
    first = ((z + 4 - y) % 4) * 2 + xh
    mirror = 2 * z + xl
    shifted = ((z + y) % 4) * 2 + xh
    own = jnp.logical_and(first == i, mirror == t)

    def seq_peer(k):
        return (k, t)

    def tensor_peer(k):
        return (s, k)

    fetch = [
        pltpu.make_async_copy(tok_hbm, tok, in_sem.at[0]),
        pltpu.make_async_copy(gain_hbm, gain, in_sem.at[1]),
        pltpu.make_async_copy(weight_hbm, weight, in_sem.at[2]),
    ]
    for copy in fetch:
        copy.start()

    barrier = pltpu.get_barrier_semaphore()
    for d in range(1, 16):
        pl.semaphore_signal(barrier, inc=1, device_id=seq_peer((s + d) % 16), device_id_type=MESH)
    for d in range(1, 8):
        pl.semaphore_signal(barrier, inc=1, device_id=tensor_peer((t + d) % 8), device_id_type=MESH)

    @pl.when(xl != xh)
    def _():
        for c in range(2):
            pl.semaphore_signal(barrier, inc=1, device_id=(2 * first + c, mirror), device_id_type=MESH)

    fetch[0].wait()
    fetch[1].wait()
    quarter = index[0] % 4
    mine = index[0] // 4 == t
    chosen = [jnp.zeros((128, 128), F32) for _ in range(4)]
    part_sq = jnp.zeros((128, 128), F32)
    for b in range(16):
        piece = tok[:, b * 128 : (b + 1) * 128].astype(F32)
        part_sq = part_sq + piece * piece
        flipped[b * 128 : (b + 1) * 128, :] = jnp.transpose(piece).astype(BF16)
        taken = jnp.logical_and(mine, quarter == b // 4)
        chosen[b % 4] = chosen[b % 4] + jnp.where(taken, piece, 0.0)
    for b in range(4):
        masked[:, b * 128 : (b + 1) * 128] = chosen[b].astype(BF16)
    taken = jnp.zeros((1, 512), F32)
    for b in range(4):
        taken = taken + jnp.where(jnp.logical_and(mine, quarter == b), gain[:, b * 512 : (b + 1) * 512], 0.0)
    gain_own[...] = jnp.broadcast_to(taken, (8, 512))
    squares[0] = lax.dot_general(
        jnp.ones((8, 128), F32), part_sq, (((1,), (1,)), ((), ())),
        precision=lax.Precision.HIGHEST, preferred_element_type=F32,
    )

    pl.semaphore_wait(barrier, jnp.where(xl == xh, 22, 24))

    def remote(src, dst, send, recv, device):
        return pltpu.make_async_remote_copy(
            src_ref=src, dst_ref=dst, send_sem=send, recv_sem=recv, device_id=device, device_id_type=MESH
        )

    def exchange(count, src, dst, send, recv, peer):
        copies = [remote(src(d), dst(d), send.at[d], recv.at[d], peer(d)) for d in range(1, count)]
        for copy in copies:
            copy.start()
        return copies

    def piece_rows(k):
        return pl.ds(pl.multiple_of(k * 16, 16), 16)

    def across(d):
        return tensor_peer((t + d) % 8)

    def along(d):
        return seq_peer((s + d) % 16)

    sq = exchange(8, lambda d: squares.at[0], lambda d: squares.at[d], sq_send, sq_recv, across)
    rs = exchange(8, lambda d: masked.at[piece_rows((t + d) % 8)], lambda d: sums.at[d], rs_send, rs_recv, across)
    gt = exchange(8, lambda d: gain_own, lambda d: gain_t.at[d], gt_send, gt_recv, across)
    def quarter_of(src, c, q):
        return src.at[pl.ds(c * 1024 + q * 512, 512)]

    def landing(chunk, c, q):
        return rows.at[chunk, c, pl.ds(q * 512, 512)]

    def into_rows(c, q, src):
        sem = 2 * q + c
        return remote(
            quarter_of(src, c, q), landing(i, core, q), x_send.at[sem], x_recv.at[2 * q + core], (2 * first + c, mirror)
        )

    def to_shifted(c, q):
        sem = 2 * q + c
        return remote(quarter_of(flipped, c, q), quarter_of(relay, c, q), y_send.at[sem], y_recv.at[sem], tensor_peer(shifted))

    def gain_to_shifted():
        return remote(gain, gain_far, y_send.at[4], y_recv.at[4], tensor_peer(shifted))

    def shift_start(q):
        @pl.when(y != 0)
        def _():
            if q == 0:
                gain_to_shifted().start()
            else:
                for c in range(2):
                    to_shifted(c, 0).wait_send()
            for c in range(2):
                to_shifted(c, q).start()

    def to_mirror(src, gains, q):
        for c in range(2):
            @pl.loop(0, 4)
            def _(b):
                at = pl.ds(pl.multiple_of(c * 1024 + q * 512 + b * 128, 128), 128)
                by_row = jnp.transpose(jnp.broadcast_to(gains[:, at], (128, 128)))
                by_lane = jnp.broadcast_to(scale_lanes[0:1, :], (128, 128))
                src[at, :] = (src[at, :].astype(F32) * by_lane * by_row * (1.0 / TOKENS)).astype(BF16)

            keeps = jnp.logical_and(own, core == c)

            @pl.when(keeps)
            def _():
                pltpu.make_async_copy(quarter_of(src, c, q), landing(i, core, q), x_local.at[q]).start()

            @pl.when(jnp.logical_not(keeps))
            def _():
                into_rows(c, q, src).start()

    def relay_on(q):
        @pl.when(y == 0)
        def _():
            to_mirror(flipped, gain, q)

        @pl.when(y != 0)
        def _():
            if q == 0:
                gain_to_shifted().wait_recv()
            for c in range(2):
                to_shifted(c, q).wait_recv()
            to_mirror(relay, gain_far, q)

    def landed_rows(q):
        for c in range(2):
            @pl.when(jnp.logical_not(jnp.logical_and(own, core == c)))
            def _():
                there = landing(first, c, q)
                remote(there, there, x_send.at[0], x_recv.at[2 * q + c], seq_peer(s + 1 - 2 * core)).wait_recv()

        @pl.when(own)
        def _():
            pltpu.make_async_copy(quarter_of(flipped, 0, q), landing(i, core, q), x_local.at[q]).wait()

    shift_start(0)
    for copy in sq:
        copy.wait_recv()
    total = squares[0]
    for d in range(1, 8):
        total = total + squares[d]
    scale = lax.rsqrt(total / D + EPSILON)
    scale_lanes[...] = scale
    scale = jnp.transpose(jnp.broadcast_to(scale[0:1, :], (128, 128)))
    scales[...] = scale
    shift_start(1)

    for copy in rs + gt:
        copy.wait_recv()
    total = masked[piece_rows(t), :].astype(F32)
    total_gain = gain_own[0:1, :]
    for d in range(1, 8):
        total = total + sums[d].astype(F32)
        total_gain = total_gain + gain_t[d, 0:1, :]

    def panel_piece(k):
        return panel.at[i, pl.ds(pl.multiple_of(core * 128 + k * 16, 16), 16), :]

    piece_scale = scales[piece_rows(t), :]
    for b in range(4):
        lanes = slice(b * 128, (b + 1) * 128)
        panel[i, pl.ds(pl.multiple_of(core * 128 + t * 16, 16), 16), lanes] = (
            total[:, lanes] * piece_scale * total_gain[:, lanes]
        ).astype(BF16)
    ag = [remote(panel_piece(t), panel_piece(t), ag_send.at[d], ag_recv.at[d], across(d)) for d in range(1, 8)]
    for copy in ag:
        copy.start()

    relay_on(0)
    own_rows = pl.ds(pl.multiple_of(core * 128, 128), 128)
    trace = jnp.zeros((128, 128), F32)
    for b in range(16):
        lanes = slice(b * 128, (b + 1) * 128)
        scaled = tok[:, lanes].astype(F32) * scale * gain[:, lanes]
        rounded = scaled.astype(BF16)
        cols[i, own_rows, lanes] = rounded
        wide = rounded.astype(F32)
        trace = trace + wide * wide
    trace_own[...] = jnp.sum(trace.reshape(16, 8, 128), axis=0)
    tt = exchange(8, lambda d: trace_own, lambda d: trace_t.at[d], tt_send, tt_recv, across)

    class Ring:
        ITEMS = ("B", "A-", "A+", "B-", "B+", "A--", "B++", "C-", "C+", "C--")
        AT = {
            "A": (0, 0), "B": (0, 1), "A-": (-1, 0), "A+": (1, 0), "B-": (-1, 1), "B+": (1, 1), "A--": (-2, 0), "B++": (2, 1),
            "C-": (-1, 1), "C+": (1, 1), "C--": (2, 1),
        }

        def __init__(self, slot, send, recv, partner, up, down, sibling, split=None):
            self.slot, self.send, self.recv, self.split = slot, send, recv, split
            self.peers = {"X": partner, "P": up, "M": down, "S": sibling}
            self.sent = []

        def part(self, kind):
            if self.split is None:
                return None
            return {"A": None, "B": (0, self.split), "C": (self.split, 128)}[kind]

        def copy(self, item, peer, lands):
            k = (11 if lands[0] == "S" else 0) + (("A",) + self.ITEMS).index(lands.lstrip("S"))
            kind = lands.lstrip("S")[0]
            ref = self.slot(*self.AT[item], rows=None if lands.lstrip("S") == "B" else self.part(kind))
            return remote(ref, ref, self.send.at[k], self.recv.at[k], self.peers[peer])

        def go(self, item, *targets):
            if self.peers["S"] is not None:
                targets = targets + (("S", "S" + item),)
            for peer, lands in targets:
                self.copy(item, peer, lands).start()
                self.sent.append((item, peer, lands))

        def wait(self, item):
            k = (11 if item[0] == "S" else 0) + (("A",) + self.ITEMS).index(item.lstrip("S"))
            name = item.lstrip("S")
            ref = self.slot(*self.AT[name], flip=item[0] == "S", rows=None if name == "B" else self.part(name[0]))
            remote(ref, ref, self.send.at[k], self.recv.at[k], self.peers["P"]).wait_recv()

        def across(self, lands):
            return () if self.split is None else (("X", lands),)

        def step0(self):
            self.go("A", ("P", "A-"), ("M", "A+"), ("X", "B"))

        def step1(self):
            self.wait("B")
            self.go("B", ("P", "B-"), ("M", "B+"))

        def step2(self):
            self.wait("A-")
            self.go("A-", ("P", "A--"), *self.across("C-"))
            self.wait("A+")
            self.go("A+", *self.across("C+"))

        def step3(self):
            self.wait("B+")
            self.go("B+", ("M", "B++"))
            self.wait("B-")
            self.go("B-")
            if self.split is not None:
                self.wait("C-")
                self.go("C-")
                self.wait("C+")
                self.go("C+")

        def step4(self):
            self.wait("A--")
            self.go("A--", *self.across("C--"))
            self.wait("B++")
            self.go("B++")

        def step5(self):
            self.wait("C--")
            self.go("C--")

        def siblings(self, *items):
            for item in items:
                self.wait("S" + item)

        def drain(self):
            for sent in self.sent:
                self.copy(*sent).wait_send()

    def half_slot(buffer):
        def slot(dy, dx, flip=False, rows=None):
            low, high = rows or (0, 128)
            chunk = ((y + dy + 4) % 4) * 2 + (xl + dx) % 2
            half = (1 - core) if flip else core
            return buffer.at[chunk, pl.ds(pl.multiple_of(half * 128 + low, 16), high - low), :]
        return slot

    def row_slot(dz, dx, **_):
        return rows.at[((z + 8 + dz - y) % 4) * 2 + (xh + dx) % 2]

    def row_part(q):
        return lambda dz, dx, **_: row_slot(dz, dx).at[:, pl.ds(q * 512, 512)]

    seq_ring = (seq_peer(s + 2 - 4 * xl), seq_peer((s + 4) % 16), seq_peer((s + 12) % 16), seq_peer(s + 1 - 2 * core))
    c_ring = Ring(half_slot(cols), c_send, c_recv, *seq_ring, split=80)
    p_ring = Ring(half_slot(panel), p_send, p_recv, *seq_ring)
    z_ring = (tensor_peer(t + 1 - 2 * xh), tensor_peer((t + 2) % 8), tensor_peer((t + 6) % 8), None)
    r_ring = [Ring(row_part(q), r_send.at[q], r_recv.at[q], *z_ring) for q in range(2)]

    for d in range(1, 8):
        there = panel_piece((t + 8 - d) % 8)
        remote(there, there, ag_send.at[d], ag_recv.at[d], across(d)).wait_recv()
    p_ring.step0()

    for copy in tt:
        copy.wait_recv()
    total = trace_own[...]
    for d in range(1, 8):
        total = total + trace_t[d]
    trace_sum[...] = total
    ts = exchange(16, lambda d: trace_sum, lambda d: trace_s.at[d], ts_send, ts_recv, along)
    p_ring.step1()
    relay_on(1)
    p_ring.step2()
    p_ring.step3()
    c_ring.step0()
    landed_rows(0)
    r_ring[0].step0()
    p_ring.step4()
    p_ring.siblings("A", "B", "A-", "A+", "B-", "B+", "A--", "B++")

    for copy in ts:
        copy.wait_recv()
    total = trace_sum[...]
    for d in range(1, 16):
        total = total + trace_s[d]
    shift = DAMPING * (jnp.sum(total) / TOKENS) / D

    def fill(b, _):
        at = pl.ds(pl.multiple_of(b * 128, 128), 128)
        block = jnp.zeros((128, 512), F32)
        for k in range(8):
            block = block + dot(panel[k, :, at], panel[k], ((0,), (0,)))
        eye = (
            b * 128 + lax.broadcasted_iota(jnp.int32, (128, 512), 0)
            == lax.broadcasted_iota(jnp.int32, (128, 512), 1)
        )
        ext[at, 0:512] = block * (1.0 / TOKENS) + jnp.where(eye, shift, 0.0)
        ext[at, 512:1024] = jnp.where(eye, 1.0, 0.0)
        return 0

    lax.fori_loop(0, 4, fill, 0)
    landed_rows(1)
    r_ring[1].step0()
    c_ring.step1()

    far = (y + 2) % 4
    apart = (z + 8 - 2 * y) % 4
    early = [(far + jnp.where(apart >= 2, 1, 2)) % 4, (far + jnp.where(apart == 3, 2, 3)) % 4]
    late = [far, (far + jnp.where(apart == 0, 1, apart)) % 4]

    def row_band(k, band):
        return jnp.concatenate([rows[k, 0, band, :], rows[k, 1, band, :]], axis=1)

    def product(chunks, band, right_of):
        total = None
        for ky in chunks:
            for kx in range(2):
                k = ky * 2 + kx
                term = dot(row_band(k, band), right_of(k), ((1,), (0,)))
                total = term if total is None else total + term
        return total

    def gram_band(chunks, band):
        for n in range(4):
            lanes = slice(n * 512, (n + 1) * 512)
            yield lanes, product(chunks, band, lambda k: cols[k, :, lanes])

    def factor(b):
        base = b * 128
        at = pl.ds(pl.multiple_of(base, 128), 128)
        tiles = [ext[pl.ds(pl.multiple_of(base + 8 * g, 8), 8), at] for g in range(16)]
        inv = jnp.concatenate(inverse_factor(tiles), axis=0)
        upper = dot_split(inv, ext[at, :], ((1,), (0,)))
        inverse[at, :] = upper[:, 512:1024]
        above[...] = upper

        def below(k, _):
            lanes = pl.ds(pl.multiple_of(k * 128, 128), 128)
            ext[lanes, :] = ext[lanes, :] - dot_split(above[:, lanes], above[...], ((0,), (0,)))
            return 0

        lax.fori_loop(b + 1, 4, below, 0)

    def factor_and_forward(b, _):
        factor(b)

        @pl.when(b == 0)
        def _():
            r_ring[0].step1()
            c_ring.step2()
            r_ring[0].step2()

        @pl.when(b == 1)
        def _():
            r_ring[1].step1()
            c_ring.step3()
            r_ring[1].step2()

        @pl.when(b == 2)
        def _():
            r_ring[0].step3()
            r_ring[1].step3()
            c_ring.step4()

        @pl.when(b == 3)
        def _():
            c_ring.step5()

        return 0

    lax.fori_loop(0, 4, factor_and_forward, 0)
    c_ring.siblings("A", "B", "A-", "A+", "B-", "B+", "C-", "C+")

    @pl.loop(0, 1024 // BAND)
    def _(m):
        band = pl.ds(pl.multiple_of(m * BAND, BAND), BAND)
        right[band, :] = product(early, band, lambda k: panel[k])
        for lanes, value in gram_band(early, band):
            gram[band, lanes] = value

    for ring in r_ring:
        ring.wait("A--")
        ring.wait("B++")

    @pl.loop(0, 1024 // BAND)
    def _(m):
        band = pl.ds(pl.multiple_of(m * BAND, BAND), BAND)
        at = s * 1024 + m * BAND - start
        eye = at + lax.broadcasted_iota(jnp.int32, (BAND, 512), 0) == lax.broadcasted_iota(jnp.int32, (BAND, 512), 1)
        block = right[band, :] + product(late, band, lambda k: panel[k]) + jnp.where(eye, shift, 0.0)
        white[band, :] = dot_split(block, inverse[...], ((1,), (1,))).astype(BF16)

    fetch[2].wait()
    for k in range(4):
        lanes = slice(k * 128, (k + 1) * 128)
        part[lanes, :] = dot(white[:, lanes], weight[...], ((0,), (1,)))

    def part_rows(k):
        return part.at[pl.ds(pl.multiple_of(k * 32, 32), 32)]

    fs = exchange(16, lambda d: part_rows((s + d) % 16), lambda d: landed.at[d], f_send, f_recv, along)
    c_ring.siblings("A--", "B++", "C--")

    @pl.loop(0, 1024 // BAND)
    def _(m):
        band = pl.ds(pl.multiple_of(m * BAND, BAND), BAND)
        for lanes, value in gram_band(late, band):
            gram[band, lanes] = gram[band, lanes] + value

    @pl.when(i == t)
    def _():
        @pl.loop(0, 8)
        def _(m):
            band = pl.ds(pl.multiple_of(m * 128, 128), 128)
            at = pl.ds(pl.multiple_of(core * 1024 + m * 128, 128), 128)
            eye = lax.broadcasted_iota(jnp.int32, (128, 128), 0) == lax.broadcasted_iota(jnp.int32, (128, 128), 1)
            gram[band, at] += jnp.where(eye, shift, 0.0)

    for copy in fs:
        copy.wait_recv()
    total = part[pl.ds(pl.multiple_of(s * 32, 32), 32), :]
    for d in range(1, 16):
        total = total + landed[d]
    proj_out[...] = total

    for copies in (sq, rs, gt, tt, ag, ts, fs):
        for copy in copies:
            copy.wait_send()
    for ring in (p_ring, c_ring, *r_ring):
        ring.drain()
    for c in range(2):
        @pl.when(jnp.logical_not(jnp.logical_and(own, core == c)))
        def _():
            for q in range(2):
                into_rows(c, q, flipped).wait_send()

        @pl.when(y != 0)
        def _():
            to_shifted(c, 1).wait_send()

    @pl.when(y != 0)
    def _():
        gain_to_shifted().wait_send()


def on_device(tokens, norm_gain, projection_weight, panel_index):
    vmem = pl.BlockSpec(memory_space=pltpu.VMEM)
    hbm = pl.BlockSpec(memory_space=pltpu.HBM)
    dma = pltpu.SemaphoreType.DMA
    gram, white, projected = pl.pallas_call(
        kernel,
        out_shape=(
            jax.ShapeDtypeStruct((1024, 2048), F32),
            jax.ShapeDtypeStruct((1024, 512), BF16),
            jax.ShapeDtypeStruct((32, 256), F32),
        ),
        in_specs=[hbm, hbm, pl.BlockSpec(memory_space=pltpu.SMEM), hbm],
        out_specs=(vmem, vmem, vmem),
        scratch_shapes=[
            pltpu.VMEM((128, 2048), BF16),
            pltpu.VMEM((1, 2048), F32),
            pltpu.VMEM((256, 1024), BF16),
            pltpu.VMEM((8, 256, 2048), BF16),
            pltpu.VMEM((8, 2, 1024, 128), BF16),
            pltpu.VMEM((8, 256, 512), BF16),
            pltpu.VMEM((512, 1024), F32),
            pltpu.VMEM((512, 512), F32),
            pltpu.VMEM((512, 256), F32),
            pltpu.VMEM((16, 32, 256), F32),
            pltpu.VMEM((2048, 128), BF16),
            pltpu.VMEM((8, 8, 128), F32),
            pltpu.VMEM((128, 512), BF16),
            pltpu.VMEM((8, 16, 512), BF16),
            pltpu.VMEM((8, 512), F32),
            pltpu.VMEM((8, 8, 512), F32),
            pltpu.VMEM((128, 128), F32),
            pltpu.VMEM((8, 128), F32),
            pltpu.VMEM((8, 8, 128), F32),
            pltpu.VMEM((16, 8, 128), F32),
            pltpu.VMEM((8, 128), F32),
            dma((3,)),
            dma((8,)), dma((8,)), dma((8,)), dma((8,)), dma((8,)), dma((8,)),
            dma((8,)), dma((8,)), dma((8,)), dma((8,)), dma((16,)), dma((16,)),
            dma((22,)), dma((22,)), dma((22,)), dma((22,)), dma((2, 22)), dma((2, 22)), dma((4,)), dma((4,)), dma((2,)), dma((5,)), dma((5,)),
            pltpu.VMEM((2048, 128), BF16), pltpu.VMEM((1, 2048), F32), pltpu.VMEM((8, 128), F32),
            pltpu.VMEM((1024, 512), F32), pltpu.VMEM((128, 1024), F32), dma((16,)), dma((16,)),
        ],
        compiler_params=pltpu.CompilerParams(
            collective_id=0, has_side_effects=True, vmem_limit_bytes=36 * 1024 * 1024
        ),
        cost_estimate=pl.CostEstimate(flops=12_000_000_000, bytes_accessed=20_000_000, transcendentals=0),
        name="whiten",
    )(tokens, norm_gain[None, :], panel_index, projection_weight)
    return gram, white, projected.T


def solution(mesh):
    placed = (P("seq", "tensor"), P("tensor"), P("tensor", "seq"), P())
    return jax.shard_map(
        on_device,
        mesh=mesh,
        in_specs=placed,
        out_specs=(P("seq", "tensor"), P("seq", None), P("tensor", "seq")),
        check_vma=False,
    )
```

```python
import functools

import jax
import jax.numpy as jnp
from jax import lax
from jax.experimental import pallas as pl
from jax.experimental.pallas import tpu as pltpu
from jax.sharding import PartitionSpec as P

D = 16384
PANEL = 512
TOKENS = 2048
EPSILON = 1e-05
DAMPING = 0.1
BAND = 512
F32 = jnp.float32
BF16 = jnp.bfloat16
MESH = pl.DeviceIdType.MESH


def halves(a):
    high = a.astype(BF16)
    return high, (a - high.astype(F32)).astype(BF16)


def dot(a, b, dims):
    return lax.dot_general(a, b, (dims, ((), ())), preferred_element_type=F32)


def dot_split(a, b, dims):
    ah, al = halves(a)
    bh, bl = halves(b)
    return dot(ah, bh, dims) + (dot(ah, bl, dims) + dot(al, bh, dims))


def row_of(tile, r):
    return jnp.broadcast_to(tile[r : r + 1, :], (8, 128))


def column_of(tile, k):
    return jnp.broadcast_to(tile[:, k : k + 1], (8, 128))


def inverse_factor(a):
    sub = lax.broadcasted_iota(jnp.int32, (8, 128), 0)
    lane = lax.broadcasted_iota(jnp.int32, (8, 128), 1)
    inv = [jnp.where(sub + 8 * g == lane, 1.0, 0.0).astype(F32) for g in range(16)]
    for g in range(16):
        cols = [{k: column_of(a[k], 8 * g + c) for k in range(g, 16)} for c in range(8)]
        for c in range(8):
            r = lax.rsqrt(row_of(cols[c][g], c))
            m = {k: cols[c][k] * r for k in range(g, 16)}
            for c2 in range(c + 1, 8):
                f = row_of(cols[c2][g], c) * r
                for k in range(g, 16):
                    cols[c2][k] = cols[c2][k] - m[k] * f
            u = row_of(a[g], c) * r
            z = row_of(inv[g], c) * r
            m[g] = jnp.where(sub > c, m[g], 0.0)
            for k in range(g, 16):
                a[k] = a[k] - m[k] * u
                inv[k] = inv[k] - m[k] * z
            inv[g] = jnp.where(sub == c, z, inv[g])
    return inv


def kernel(
    tok_hbm, gain_hbm, index, weight_hbm,
    gram, white, proj_out,
    tok, gain, weight, cols, rows, panel, ext, inverse, part, landed,
    flipped, squares, masked, sums, gain_own, gain_t, scales, trace_own, trace_t, trace_s, trace_sum,
    in_sem, sq_send, sq_recv, rs_send, rs_recv, gt_send, gt_recv, ag_send, ag_recv, tt_send, tt_recv, ts_send, ts_recv,
    p_send, p_recv, c_send, c_recv, r_send, r_recv, x_send, x_recv, x_local, y_send, y_recv, relay, gain_far, scale_lanes, right, above, f_send, f_recv,
):
    s, t = lax.axis_index("seq"), lax.axis_index("tensor")
    i, core = s // 2, s % 2
    y, xl = i // 2, i % 2
    z, xh = t // 2, t % 2
    start = index[0] * PANEL
    first = ((z + 4 - y) % 4) * 2 + xh
    mirror = 2 * z + xl
    shifted = ((z + y) % 4) * 2 + xh
    own = jnp.logical_and(first == i, mirror == t)

    def seq_peer(k):
        return (k, t)

    def tensor_peer(k):
        return (s, k)

    fetch = [
        pltpu.make_async_copy(tok_hbm, tok, in_sem.at[0]),
        pltpu.make_async_copy(gain_hbm, gain, in_sem.at[1]),
        pltpu.make_async_copy(weight_hbm, weight, in_sem.at[2]),
    ]
    for copy in fetch:
        copy.start()

    barrier = pltpu.get_barrier_semaphore()
    for d in range(1, 16):
        pl.semaphore_signal(barrier, inc=1, device_id=seq_peer((s + d) % 16), device_id_type=MESH)
    for d in range(1, 8):
        pl.semaphore_signal(barrier, inc=1, device_id=tensor_peer((t + d) % 8), device_id_type=MESH)

    @pl.when(xl != xh)
    def _():
        for c in range(2):
            pl.semaphore_signal(barrier, inc=1, device_id=(2 * first + c, mirror), device_id_type=MESH)

    fetch[0].wait()
    fetch[1].wait()
    quarter = index[0] % 4
    mine = index[0] // 4 == t
    chosen = [jnp.zeros((128, 128), F32) for _ in range(4)]
    part_sq = jnp.zeros((128, 128), F32)
    for b in range(16):
        piece = tok[:, b * 128 : (b + 1) * 128].astype(F32)
        part_sq = part_sq + piece * piece
        flipped[b * 128 : (b + 1) * 128, :] = jnp.transpose(piece).astype(BF16)
        taken = jnp.logical_and(mine, quarter == b // 4)
        chosen[b % 4] = chosen[b % 4] + jnp.where(taken, piece, 0.0)
    for b in range(4):
        masked[:, b * 128 : (b + 1) * 128] = chosen[b].astype(BF16)
    taken = jnp.zeros((1, 512), F32)
    for b in range(4):
        taken = taken + jnp.where(jnp.logical_and(mine, quarter == b), gain[:, b * 512 : (b + 1) * 512], 0.0)
    gain_own[...] = jnp.broadcast_to(taken, (8, 512))
    squares[0] = lax.dot_general(
        jnp.ones((8, 128), F32), part_sq, (((1,), (1,)), ((), ())),
        precision=lax.Precision.HIGHEST, preferred_element_type=F32,
    )

    pl.semaphore_wait(barrier, jnp.where(xl == xh, 22, 24))

    def remote(src, dst, send, recv, device):
        return pltpu.make_async_remote_copy(
            src_ref=src, dst_ref=dst, send_sem=send, recv_sem=recv, device_id=device, device_id_type=MESH
        )

    def exchange(count, src, dst, send, recv, peer):
        copies = [remote(src(d), dst(d), send.at[d], recv.at[d], peer(d)) for d in range(1, count)]
        for copy in copies:
            copy.start()
        return copies

    def piece_rows(k):
        return pl.ds(pl.multiple_of(k * 16, 16), 16)

    def across(d):
        return tensor_peer((t + d) % 8)

    def along(d):
        return seq_peer((s + d) % 16)

    sq = exchange(8, lambda d: squares.at[0], lambda d: squares.at[d], sq_send, sq_recv, across)
    rs = exchange(8, lambda d: masked.at[piece_rows((t + d) % 8)], lambda d: sums.at[d], rs_send, rs_recv, across)
    gt = exchange(8, lambda d: gain_own, lambda d: gain_t.at[d], gt_send, gt_recv, across)
    def quarter_of(src, c, q):
        return src.at[pl.ds(c * 1024 + q * 512, 512)]

    def landing(chunk, c, q):
        return rows.at[chunk, c, pl.ds(q * 512, 512)]

    def into_rows(c, q, src):
        sem = 2 * q + c
        return remote(
            quarter_of(src, c, q), landing(i, core, q), x_send.at[sem], x_recv.at[2 * q + core], (2 * first + c, mirror)
        )

    def to_shifted(c, q):
        sem = 2 * q + c
        return remote(quarter_of(flipped, c, q), quarter_of(relay, c, q), y_send.at[sem], y_recv.at[sem], tensor_peer(shifted))

    def gain_to_shifted():
        return remote(gain, gain_far, y_send.at[4], y_recv.at[4], tensor_peer(shifted))

    def shift_start(q):
        @pl.when(y != 0)
        def _():
            if q == 0:
                gain_to_shifted().start()
            else:
                for c in range(2):
                    to_shifted(c, 0).wait_send()
            for c in range(2):
                to_shifted(c, q).start()

    def to_mirror(src, gains, q):
        for c in range(2):
            @pl.loop(0, 4)
            def _(b):
                at = pl.ds(pl.multiple_of(c * 1024 + q * 512 + b * 128, 128), 128)
                by_row = jnp.transpose(jnp.broadcast_to(gains[:, at], (128, 128)))
                by_lane = jnp.broadcast_to(scale_lanes[0:1, :], (128, 128))
                src[at, :] = (src[at, :].astype(F32) * by_lane * by_row * (1.0 / TOKENS)).astype(BF16)

            keeps = jnp.logical_and(own, core == c)

            @pl.when(keeps)
            def _():
                pltpu.make_async_copy(quarter_of(src, c, q), landing(i, core, q), x_local.at[q]).start()

            @pl.when(jnp.logical_not(keeps))
            def _():
                into_rows(c, q, src).start()

    def relay_on(q):
        @pl.when(y == 0)
        def _():
            to_mirror(flipped, gain, q)

        @pl.when(y != 0)
        def _():
            if q == 0:
                gain_to_shifted().wait_recv()
            for c in range(2):
                to_shifted(c, q).wait_recv()
            to_mirror(relay, gain_far, q)

    def landed_rows(q):
        for c in range(2):
            @pl.when(jnp.logical_not(jnp.logical_and(own, core == c)))
            def _():
                there = landing(first, c, q)
                remote(there, there, x_send.at[0], x_recv.at[2 * q + c], seq_peer(s + 1 - 2 * core)).wait_recv()

        @pl.when(own)
        def _():
            pltpu.make_async_copy(quarter_of(flipped, 0, q), landing(i, core, q), x_local.at[q]).wait()

    shift_start(0)
    for copy in sq:
        copy.wait_recv()
    total = squares[0]
    for d in range(1, 8):
        total = total + squares[d]
    scale = lax.rsqrt(total / D + EPSILON)
    scale_lanes[...] = scale
    scale = jnp.transpose(jnp.broadcast_to(scale[0:1, :], (128, 128)))
    scales[...] = scale
    shift_start(1)

    for copy in rs + gt:
        copy.wait_recv()
    total = masked[piece_rows(t), :].astype(F32)
    total_gain = gain_own[0:1, :]
    for d in range(1, 8):
        total = total + sums[d].astype(F32)
        total_gain = total_gain + gain_t[d, 0:1, :]

    def panel_piece(k):
        return panel.at[i, pl.ds(pl.multiple_of(core * 128 + k * 16, 16), 16), :]

    piece_scale = scales[piece_rows(t), :]
    for b in range(4):
        lanes = slice(b * 128, (b + 1) * 128)
        panel[i, pl.ds(pl.multiple_of(core * 128 + t * 16, 16), 16), lanes] = (
            total[:, lanes] * piece_scale * total_gain[:, lanes]
        ).astype(BF16)
    ag = [remote(panel_piece(t), panel_piece(t), ag_send.at[d], ag_recv.at[d], across(d)) for d in range(1, 8)]
    for copy in ag:
        copy.start()

    relay_on(0)
    own_rows = pl.ds(pl.multiple_of(core * 128, 128), 128)
    trace = jnp.zeros((128, 128), F32)
    for b in range(16):
        lanes = slice(b * 128, (b + 1) * 128)
        scaled = tok[:, lanes].astype(F32) * scale * gain[:, lanes]
        rounded = scaled.astype(BF16)
        cols[i, own_rows, lanes] = rounded
        wide = rounded.astype(F32)
        trace = trace + wide * wide
    trace_own[...] = jnp.sum(trace.reshape(16, 8, 128), axis=0)
    tt = exchange(8, lambda d: trace_own, lambda d: trace_t.at[d], tt_send, tt_recv, across)

    class Ring:
        ITEMS = ("B", "A-", "A+", "B-", "B+", "A--", "B++", "C-", "C+", "C--")
        AT = {
            "A": (0, 0), "B": (0, 1), "A-": (-1, 0), "A+": (1, 0), "B-": (-1, 1), "B+": (1, 1), "A--": (-2, 0), "B++": (2, 1),
            "C-": (-1, 1), "C+": (1, 1), "C--": (2, 1),
        }

        def __init__(self, slot, send, recv, partner, up, down, sibling, split=None):
            self.slot, self.send, self.recv, self.split = slot, send, recv, split
            self.peers = {"X": partner, "P": up, "M": down, "S": sibling}
            self.sent = []

        def part(self, kind):
            if self.split is None:
                return None
            return {"A": None, "B": (0, self.split), "C": (self.split, 128)}[kind]

        def copy(self, item, peer, lands):
            k = (11 if lands[0] == "S" else 0) + (("A",) + self.ITEMS).index(lands.lstrip("S"))
            kind = lands.lstrip("S")[0]
            ref = self.slot(*self.AT[item], rows=None if lands.lstrip("S") == "B" else self.part(kind))
            return remote(ref, ref, self.send.at[k], self.recv.at[k], self.peers[peer])

        def go(self, item, *targets):
            if self.peers["S"] is not None:
                targets = targets + (("S", "S" + item),)
            for peer, lands in targets:
                self.copy(item, peer, lands).start()
                self.sent.append((item, peer, lands))

        def wait(self, item):
            k = (11 if item[0] == "S" else 0) + (("A",) + self.ITEMS).index(item.lstrip("S"))
            name = item.lstrip("S")
            ref = self.slot(*self.AT[name], flip=item[0] == "S", rows=None if name == "B" else self.part(name[0]))
            remote(ref, ref, self.send.at[k], self.recv.at[k], self.peers["P"]).wait_recv()

        def across(self, lands):
            return () if self.split is None else (("X", lands),)

        def step0(self):
            self.go("A", ("P", "A-"), ("M", "A+"), ("X", "B"))

        def step1(self):
            self.wait("B")
            self.go("B", ("P", "B-"), ("M", "B+"))

        def step2(self):
            self.wait("A-")
            self.go("A-", ("P", "A--"), *self.across("C-"))
            self.wait("A+")
            self.go("A+", *self.across("C+"))

        def step3(self):
            self.wait("B+")
            self.go("B+", ("M", "B++"))
            self.wait("B-")
            self.go("B-")
            if self.split is not None:
                self.wait("C-")
                self.go("C-")
                self.wait("C+")
                self.go("C+")

        def step4(self):
            self.wait("A--")
            self.go("A--", *self.across("C--"))
            self.wait("B++")
            self.go("B++")

        def step5(self):
            self.wait("C--")
            self.go("C--")

        def siblings(self, *items):
            for item in items:
                self.wait("S" + item)

        def drain(self):
            for sent in self.sent:
                self.copy(*sent).wait_send()

    def half_slot(buffer):
        def slot(dy, dx, flip=False, rows=None):
            low, high = rows or (0, 128)
            chunk = ((y + dy + 4) % 4) * 2 + (xl + dx) % 2
            half = (1 - core) if flip else core
            return buffer.at[chunk, pl.ds(pl.multiple_of(half * 128 + low, 16), high - low), :]
        return slot

    def row_slot(dz, dx, **_):
        return rows.at[((z + 8 + dz - y) % 4) * 2 + (xh + dx) % 2]

    def row_part(q):
        return lambda dz, dx, **_: row_slot(dz, dx).at[:, pl.ds(q * 512, 512)]

    seq_ring = (seq_peer(s + 2 - 4 * xl), seq_peer((s + 4) % 16), seq_peer((s + 12) % 16), seq_peer(s + 1 - 2 * core))
    c_ring = Ring(half_slot(cols), c_send, c_recv, *seq_ring, split=80)
    p_ring = Ring(half_slot(panel), p_send, p_recv, *seq_ring)
    z_ring = (tensor_peer(t + 1 - 2 * xh), tensor_peer((t + 2) % 8), tensor_peer((t + 6) % 8), None)
    r_ring = [Ring(row_part(q), r_send.at[q], r_recv.at[q], *z_ring) for q in range(2)]

    for d in range(1, 8):
        there = panel_piece((t + 8 - d) % 8)
        remote(there, there, ag_send.at[d], ag_recv.at[d], across(d)).wait_recv()
    p_ring.step0()

    for copy in tt:
        copy.wait_recv()
    total = trace_own[...]
    for d in range(1, 8):
        total = total + trace_t[d]
    trace_sum[...] = total
    ts = exchange(16, lambda d: trace_sum, lambda d: trace_s.at[d], ts_send, ts_recv, along)
    relay_on(1)
    p_ring.step1()
    p_ring.step2()
    p_ring.step3()
    c_ring.step0()
    landed_rows(0)
    r_ring[0].step0()
    p_ring.step4()
    p_ring.siblings("A", "B", "A-", "A+", "B-", "B+", "A--", "B++")

    for copy in ts:
        copy.wait_recv()
    total = trace_sum[...]
    for d in range(1, 16):
        total = total + trace_s[d]
    shift = DAMPING * (jnp.sum(total) / TOKENS) / D

    def fill(b, _):
        at = pl.ds(pl.multiple_of(b * 128, 128), 128)
        block = jnp.zeros((128, 512), F32)
        for k in range(8):
            block = block + dot(panel[k, :, at], panel[k], ((0,), (0,)))
        eye = (
            b * 128 + lax.broadcasted_iota(jnp.int32, (128, 512), 0)
            == lax.broadcasted_iota(jnp.int32, (128, 512), 1)
        )
        ext[at, 0:512] = block * (1.0 / TOKENS) + jnp.where(eye, shift, 0.0)
        ext[at, 512:1024] = jnp.where(eye, 1.0, 0.0)
        return 0

    lax.fori_loop(0, 4, fill, 0)
    landed_rows(1)
    r_ring[1].step0()
    c_ring.step1()

    far = (y + 2) % 4
    apart = (z + 8 - 2 * y) % 4
    early = [(far + jnp.where(apart >= 2, 1, 2)) % 4, (far + jnp.where(apart == 3, 2, 3)) % 4]
    late = [far, (far + jnp.where(apart == 0, 1, apart)) % 4]

    def row_band(k, band):
        return jnp.concatenate([rows[k, 0, band, :], rows[k, 1, band, :]], axis=1)

    def product(chunks, band, right_of):
        total = None
        for ky in chunks:
            for kx in range(2):
                k = ky * 2 + kx
                term = dot(row_band(k, band), right_of(k), ((1,), (0,)))
                total = term if total is None else total + term
        return total

    def gram_band(chunks, band):
        for n in range(4):
            lanes = slice(n * 512, (n + 1) * 512)
            yield lanes, product(chunks, band, lambda k: cols[k, :, lanes])

    def factor(b):
        base = b * 128
        at = pl.ds(pl.multiple_of(base, 128), 128)
        tiles = [ext[pl.ds(pl.multiple_of(base + 8 * g, 8), 8), at] for g in range(16)]
        inv = jnp.concatenate(inverse_factor(tiles), axis=0)
        upper = dot_split(inv, ext[at, :], ((1,), (0,)))
        inverse[at, :] = upper[:, 512:1024]
        above[...] = upper

        def below(k, _):
            lanes = pl.ds(pl.multiple_of(k * 128, 128), 128)
            ext[lanes, :] = ext[lanes, :] - dot_split(above[:, lanes], above[...], ((0,), (0,)))
            return 0

        lax.fori_loop(b + 1, 4, below, 0)

    def factor_and_forward(b, _):
        factor(b)

        @pl.when(b == 0)
        def _():
            r_ring[0].step1()
            c_ring.step2()
            r_ring[0].step2()

        @pl.when(b == 1)
        def _():
            r_ring[1].step1()
            c_ring.step3()
            r_ring[1].step2()

        @pl.when(b == 2)
        def _():
            r_ring[0].step3()
            r_ring[1].step3()
            c_ring.step4()

        @pl.when(b == 3)
        def _():
            c_ring.step5()

        return 0

    lax.fori_loop(0, 4, factor_and_forward, 0)
    c_ring.siblings("A", "B", "A-", "A+", "B-", "B+", "C-", "C+")

    @pl.loop(0, 1024 // BAND)
    def _(m):
        band = pl.ds(pl.multiple_of(m * BAND, BAND), BAND)
        right[band, :] = product(early, band, lambda k: panel[k])
        for lanes, value in gram_band(early, band):
            gram[band, lanes] = value

    for ring in r_ring:
        ring.wait("A--")
        ring.wait("B++")

    @pl.loop(0, 1024 // BAND)
    def _(m):
        band = pl.ds(pl.multiple_of(m * BAND, BAND), BAND)
        at = s * 1024 + m * BAND - start
        eye = at + lax.broadcasted_iota(jnp.int32, (BAND, 512), 0) == lax.broadcasted_iota(jnp.int32, (BAND, 512), 1)
        block = right[band, :] + product(late, band, lambda k: panel[k]) + jnp.where(eye, shift, 0.0)
        white[band, :] = dot_split(block, inverse[...], ((1,), (1,))).astype(BF16)

    fetch[2].wait()
    for k in range(4):
        lanes = slice(k * 128, (k + 1) * 128)
        part[lanes, :] = dot(white[:, lanes], weight[...], ((0,), (1,))).astype(BF16)

    def part_rows(k):
        return part.at[pl.ds(pl.multiple_of(k * 32, 32), 32)]

    fs = exchange(16, lambda d: part_rows((s + d) % 16), lambda d: landed.at[d], f_send, f_recv, along)
    c_ring.siblings("A--", "B++", "C--")

    @pl.loop(0, 1024 // BAND)
    def _(m):
        band = pl.ds(pl.multiple_of(m * BAND, BAND), BAND)
        for lanes, value in gram_band(late, band):
            gram[band, lanes] = gram[band, lanes] + value

    @pl.when(i == t)
    def _():
        @pl.loop(0, 8)
        def _(m):
            band = pl.ds(pl.multiple_of(m * 128, 128), 128)
            at = pl.ds(pl.multiple_of(core * 1024 + m * 128, 128), 128)
            eye = lax.broadcasted_iota(jnp.int32, (128, 128), 0) == lax.broadcasted_iota(jnp.int32, (128, 128), 1)
            gram[band, at] += jnp.where(eye, shift, 0.0)

    for copy in fs:
        copy.wait_recv()
    total = part[pl.ds(pl.multiple_of(s * 32, 32), 32), :].astype(F32)
    for d in range(1, 16):
        total = total + landed[d].astype(F32)
    proj_out[...] = total

    for copies in (sq, rs, gt, tt, ag, ts, fs):
        for copy in copies:
            copy.wait_send()
    for ring in (p_ring, c_ring, *r_ring):
        ring.drain()
    for c in range(2):
        @pl.when(jnp.logical_not(jnp.logical_and(own, core == c)))
        def _():
            for q in range(2):
                into_rows(c, q, flipped).wait_send()

        @pl.when(y != 0)
        def _():
            to_shifted(c, 1).wait_send()

    @pl.when(y != 0)
    def _():
        gain_to_shifted().wait_send()


def on_device(tokens, norm_gain, projection_weight, panel_index):
    vmem = pl.BlockSpec(memory_space=pltpu.VMEM)
    hbm = pl.BlockSpec(memory_space=pltpu.HBM)
    dma = pltpu.SemaphoreType.DMA
    gram, white, projected = pl.pallas_call(
        kernel,
        out_shape=(
            jax.ShapeDtypeStruct((1024, 2048), F32),
            jax.ShapeDtypeStruct((1024, 512), BF16),
            jax.ShapeDtypeStruct((32, 256), F32),
        ),
        in_specs=[hbm, hbm, pl.BlockSpec(memory_space=pltpu.SMEM), hbm],
        out_specs=(vmem, vmem, vmem),
        scratch_shapes=[
            pltpu.VMEM((128, 2048), BF16),
            pltpu.VMEM((1, 2048), F32),
            pltpu.VMEM((256, 1024), BF16),
            pltpu.VMEM((8, 256, 2048), BF16),
            pltpu.VMEM((8, 2, 1024, 128), BF16),
            pltpu.VMEM((8, 256, 512), BF16),
            pltpu.VMEM((512, 1024), F32),
            pltpu.VMEM((512, 512), F32),
            pltpu.VMEM((512, 256), BF16),
            pltpu.VMEM((16, 32, 256), BF16),
            pltpu.VMEM((2048, 128), BF16),
            pltpu.VMEM((8, 8, 128), F32),
            pltpu.VMEM((128, 512), BF16),
            pltpu.VMEM((8, 16, 512), BF16),
            pltpu.VMEM((8, 512), F32),
            pltpu.VMEM((8, 8, 512), F32),
            pltpu.VMEM((128, 128), F32),
            pltpu.VMEM((8, 128), F32),
            pltpu.VMEM((8, 8, 128), F32),
            pltpu.VMEM((16, 8, 128), F32),
            pltpu.VMEM((8, 128), F32),
            dma((3,)),
            dma((8,)), dma((8,)), dma((8,)), dma((8,)), dma((8,)), dma((8,)),
            dma((8,)), dma((8,)), dma((8,)), dma((8,)), dma((16,)), dma((16,)),
            dma((22,)), dma((22,)), dma((22,)), dma((22,)), dma((2, 22)), dma((2, 22)), dma((4,)), dma((4,)), dma((2,)), dma((5,)), dma((5,)),
            pltpu.VMEM((2048, 128), BF16), pltpu.VMEM((1, 2048), F32), pltpu.VMEM((8, 128), F32),
            pltpu.VMEM((1024, 512), F32), pltpu.VMEM((128, 1024), F32), dma((16,)), dma((16,)),
        ],
        compiler_params=pltpu.CompilerParams(
            collective_id=0, has_side_effects=True, vmem_limit_bytes=36 * 1024 * 1024
        ),
        cost_estimate=pl.CostEstimate(flops=12_000_000_000, bytes_accessed=20_000_000, transcendentals=0),
        name="whiten",
    )(tokens, norm_gain[None, :], panel_index, projection_weight)
    return gram, white, projected.T


def solution(mesh):
    placed = (P("seq", "tensor"), P("tensor"), P("tensor", "seq"), P())
    return jax.shard_map(
        on_device,
        mesh=mesh,
        in_specs=placed,
        out_specs=(P("seq", "tensor"), P("seq", None), P("tensor", "seq")),
        check_vma=False,
    )
```

```python
import functools

import jax
import jax.numpy as jnp
from jax import lax
from jax.experimental import pallas as pl
from jax.experimental.pallas import tpu as pltpu
from jax.sharding import PartitionSpec as P

D = 16384
PANEL = 512
TOKENS = 2048
EPSILON = 1e-05
DAMPING = 0.1
BAND = 512
F32 = jnp.float32
BF16 = jnp.bfloat16
MESH = pl.DeviceIdType.MESH


def halves(a):
    high = a.astype(BF16)
    return high, (a - high.astype(F32)).astype(BF16)


def dot(a, b, dims):
    return lax.dot_general(a, b, (dims, ((), ())), preferred_element_type=F32)


def dot_split(a, b, dims):
    ah, al = halves(a)
    bh, bl = halves(b)
    return dot(ah, bh, dims) + (dot(ah, bl, dims) + dot(al, bh, dims))


def row_of(tile, r):
    return jnp.broadcast_to(tile[r : r + 1, :], (8, 128))


def column_of(tile, k):
    return jnp.broadcast_to(tile[:, k : k + 1], (8, 128))


def inverse_factor(a):
    sub = lax.broadcasted_iota(jnp.int32, (8, 128), 0)
    lane = lax.broadcasted_iota(jnp.int32, (8, 128), 1)
    inv = [jnp.where(sub + 8 * g == lane, 1.0, 0.0).astype(F32) for g in range(16)]
    for g in range(16):
        cols = [{k: column_of(a[k], 8 * g + c) for k in range(g, 16)} for c in range(8)]
        for c in range(8):
            r = lax.rsqrt(row_of(cols[c][g], c))
            m = {k: cols[c][k] * r for k in range(g, 16)}
            for c2 in range(c + 1, 8):
                f = row_of(cols[c2][g], c) * r
                for k in range(g, 16):
                    cols[c2][k] = cols[c2][k] - m[k] * f
            u = row_of(a[g], c) * r
            z = row_of(inv[g], c) * r
            m[g] = jnp.where(sub > c, m[g], 0.0)
            for k in range(g, 16):
                a[k] = a[k] - m[k] * u
                inv[k] = inv[k] - m[k] * z
            inv[g] = jnp.where(sub == c, z, inv[g])
    return inv


def kernel(
    tok_hbm, gain_hbm, index, weight_hbm,
    gram, white, proj_out,
    tok, gain, weight, cols, rows, panel, ext, inverse, part, landed,
    flipped, squares, masked, sums, gain_own, gain_t, scales, trace_own, trace_t, trace_s, trace_sum,
    in_sem, sq_send, sq_recv, rs_send, rs_recv, gt_send, gt_recv, ag_send, ag_recv, tt_send, tt_recv, ts_send, ts_recv,
    p_send, p_recv, c_send, c_recv, r_send, r_recv, x_send, x_recv, x_local, y_send, y_recv, relay, gain_far, scale_lanes, right, above, f_send, f_recv,
):
    s, t = lax.axis_index("seq"), lax.axis_index("tensor")
    i, core = s // 2, s % 2
    y, xl = i // 2, i % 2
    z, xh = t // 2, t % 2
    start = index[0] * PANEL
    first = ((z + 4 - y) % 4) * 2 + xh
    mirror = 2 * z + xl
    shifted = ((z + y) % 4) * 2 + xh
    own = jnp.logical_and(first == i, mirror == t)

    def seq_peer(k):
        return (k, t)

    def tensor_peer(k):
        return (s, k)

    fetch = [
        pltpu.make_async_copy(tok_hbm, tok, in_sem.at[0]),
        pltpu.make_async_copy(gain_hbm, gain, in_sem.at[1]),
        pltpu.make_async_copy(weight_hbm, weight, in_sem.at[2]),
    ]
    for copy in fetch:
        copy.start()

    barrier = pltpu.get_barrier_semaphore()
    for d in range(1, 16):
        pl.semaphore_signal(barrier, inc=1, device_id=seq_peer((s + d) % 16), device_id_type=MESH)
    for d in range(1, 8):
        pl.semaphore_signal(barrier, inc=1, device_id=tensor_peer((t + d) % 8), device_id_type=MESH)

    @pl.when(xl != xh)
    def _():
        for c in range(2):
            pl.semaphore_signal(barrier, inc=1, device_id=(2 * first + c, mirror), device_id_type=MESH)

    fetch[0].wait()
    fetch[1].wait()
    quarter = index[0] % 4
    mine = index[0] // 4 == t
    chosen = [jnp.zeros((128, 128), F32) for _ in range(4)]
    part_sq = jnp.zeros((128, 128), F32)
    for b in range(16):
        piece = tok[:, b * 128 : (b + 1) * 128].astype(F32)
        part_sq = part_sq + piece * piece
        flipped[b * 128 : (b + 1) * 128, :] = jnp.transpose(piece).astype(BF16)
        taken = jnp.logical_and(mine, quarter == b // 4)
        chosen[b % 4] = chosen[b % 4] + jnp.where(taken, piece, 0.0)
    for b in range(4):
        masked[:, b * 128 : (b + 1) * 128] = chosen[b].astype(BF16)
    taken = jnp.zeros((1, 512), F32)
    for b in range(4):
        taken = taken + jnp.where(jnp.logical_and(mine, quarter == b), gain[:, b * 512 : (b + 1) * 512], 0.0)
    gain_own[...] = jnp.broadcast_to(taken, (8, 512))
    squares[0] = lax.dot_general(
        jnp.ones((8, 128), F32), part_sq, (((1,), (1,)), ((), ())),
        precision=lax.Precision.HIGHEST, preferred_element_type=F32,
    )

    pl.semaphore_wait(barrier, jnp.where(xl == xh, 22, 24))

    def remote(src, dst, send, recv, device):
        return pltpu.make_async_remote_copy(
            src_ref=src, dst_ref=dst, send_sem=send, recv_sem=recv, device_id=device, device_id_type=MESH
        )

    def exchange(count, src, dst, send, recv, peer):
        copies = [remote(src(d), dst(d), send.at[d], recv.at[d], peer(d)) for d in range(1, count)]
        for copy in copies:
            copy.start()
        return copies

    def piece_rows(k):
        return pl.ds(pl.multiple_of(k * 16, 16), 16)

    def across(d):
        return tensor_peer((t + d) % 8)

    def along(d):
        return seq_peer((s + d) % 16)

    sq = exchange(8, lambda d: squares.at[0], lambda d: squares.at[d], sq_send, sq_recv, across)
    rs = exchange(8, lambda d: masked.at[piece_rows((t + d) % 8)], lambda d: sums.at[d], rs_send, rs_recv, across)
    gt = exchange(8, lambda d: gain_own, lambda d: gain_t.at[d], gt_send, gt_recv, across)
    def quarter_of(src, c, q):
        return src.at[pl.ds(c * 1024 + q * 512, 512)]

    def landing(chunk, c, q):
        return rows.at[chunk, c, pl.ds(q * 512, 512)]

    def into_rows(c, q, src):
        sem = 2 * q + c
        return remote(
            quarter_of(src, c, q), landing(i, core, q), x_send.at[sem], x_recv.at[2 * q + core], (2 * first + c, mirror)
        )

    def to_shifted(c, q):
        sem = 2 * q + c
        return remote(quarter_of(flipped, c, q), quarter_of(relay, c, q), y_send.at[sem], y_recv.at[sem], tensor_peer(shifted))

    def gain_to_shifted():
        return remote(gain, gain_far, y_send.at[4], y_recv.at[4], tensor_peer(shifted))

    def shift_start(q):
        @pl.when(y != 0)
        def _():
            if q == 0:
                gain_to_shifted().start()
            else:
                for c in range(2):
                    to_shifted(c, 0).wait_send()
            for c in range(2):
                to_shifted(c, q).start()

    def to_mirror(src, gains, q):
        for c in range(2):
            @pl.loop(0, 4)
            def _(b):
                at = pl.ds(pl.multiple_of(c * 1024 + q * 512 + b * 128, 128), 128)
                by_row = jnp.transpose(jnp.broadcast_to(gains[:, at], (128, 128)))
                by_lane = jnp.broadcast_to(scale_lanes[0:1, :], (128, 128))
                src[at, :] = (src[at, :].astype(F32) * by_lane * by_row * (1.0 / TOKENS)).astype(BF16)

            keeps = jnp.logical_and(own, core == c)

            @pl.when(keeps)
            def _():
                pltpu.make_async_copy(quarter_of(src, c, q), landing(i, core, q), x_local.at[q]).start()

            @pl.when(jnp.logical_not(keeps))
            def _():
                into_rows(c, q, src).start()

    def relay_on(q):
        @pl.when(y == 0)
        def _():
            to_mirror(flipped, gain, q)

        @pl.when(y != 0)
        def _():
            if q == 0:
                gain_to_shifted().wait_recv()
            for c in range(2):
                to_shifted(c, q).wait_recv()
            to_mirror(relay, gain_far, q)

    def landed_rows(q):
        for c in range(2):
            @pl.when(jnp.logical_not(jnp.logical_and(own, core == c)))
            def _():
                there = landing(first, c, q)
                remote(there, there, x_send.at[0], x_recv.at[2 * q + c], seq_peer(s + 1 - 2 * core)).wait_recv()

        @pl.when(own)
        def _():
            pltpu.make_async_copy(quarter_of(flipped, 0, q), landing(i, core, q), x_local.at[q]).wait()

    shift_start(0)
    for copy in sq:
        copy.wait_recv()
    total = squares[0]
    for d in range(1, 8):
        total = total + squares[d]
    scale = lax.rsqrt(total / D + EPSILON)
    scale_lanes[...] = scale
    scale = jnp.transpose(jnp.broadcast_to(scale[0:1, :], (128, 128)))
    scales[...] = scale
    shift_start(1)

    for copy in rs + gt:
        copy.wait_recv()
    total = masked[piece_rows(t), :].astype(F32)
    total_gain = gain_own[0:1, :]
    for d in range(1, 8):
        total = total + sums[d].astype(F32)
        total_gain = total_gain + gain_t[d, 0:1, :]

    def panel_piece(k):
        return panel.at[i, pl.ds(pl.multiple_of(core * 128 + k * 16, 16), 16), :]

    piece_scale = scales[piece_rows(t), :]
    for b in range(4):
        lanes = slice(b * 128, (b + 1) * 128)
        panel[i, pl.ds(pl.multiple_of(core * 128 + t * 16, 16), 16), lanes] = (
            total[:, lanes] * piece_scale * total_gain[:, lanes]
        ).astype(BF16)
    ag = [remote(panel_piece(t), panel_piece(t), ag_send.at[d], ag_recv.at[d], across(d)) for d in range(1, 8)]
    for copy in ag:
        copy.start()

    relay_on(0)
    own_rows = pl.ds(pl.multiple_of(core * 128, 128), 128)
    trace = jnp.zeros((128, 128), F32)
    for b in range(16):
        lanes = slice(b * 128, (b + 1) * 128)
        scaled = tok[:, lanes].astype(F32) * scale * gain[:, lanes]
        rounded = scaled.astype(BF16)
        cols[i, own_rows, lanes] = rounded
        wide = rounded.astype(F32)
        trace = trace + wide * wide
    trace_own[...] = jnp.sum(trace.reshape(16, 8, 128), axis=0)
    tt = exchange(8, lambda d: trace_own, lambda d: trace_t.at[d], tt_send, tt_recv, across)

    class Ring:
        ITEMS = ("B", "A-", "A+", "B-", "B+", "A--", "B++", "C-", "C+", "C--")
        AT = {
            "A": (0, 0), "B": (0, 1), "A-": (-1, 0), "A+": (1, 0), "B-": (-1, 1), "B+": (1, 1), "A--": (-2, 0), "B++": (2, 1),
            "C-": (-1, 1), "C+": (1, 1), "C--": (2, 1),
        }

        def __init__(self, slot, send, recv, partner, up, down, sibling, split=None):
            self.slot, self.send, self.recv, self.split = slot, send, recv, split
            self.peers = {"X": partner, "P": up, "M": down, "S": sibling}
            self.sent = []

        def part(self, kind):
            if self.split is None:
                return None
            return {"A": None, "B": (0, self.split), "C": (self.split, 128)}[kind]

        def copy(self, item, peer, lands):
            k = (11 if lands[0] == "S" else 0) + (("A",) + self.ITEMS).index(lands.lstrip("S"))
            kind = lands.lstrip("S")[0]
            ref = self.slot(*self.AT[item], rows=None if lands.lstrip("S") == "B" else self.part(kind))
            return remote(ref, ref, self.send.at[k], self.recv.at[k], self.peers[peer])

        def go(self, item, *targets):
            if self.peers["S"] is not None:
                targets = targets + (("S", "S" + item),)
            for peer, lands in targets:
                self.copy(item, peer, lands).start()
                self.sent.append((item, peer, lands))

        def wait(self, item):
            k = (11 if item[0] == "S" else 0) + (("A",) + self.ITEMS).index(item.lstrip("S"))
            name = item.lstrip("S")
            ref = self.slot(*self.AT[name], flip=item[0] == "S", rows=None if name == "B" else self.part(name[0]))
            remote(ref, ref, self.send.at[k], self.recv.at[k], self.peers["P"]).wait_recv()

        def across(self, lands):
            return () if self.split is None else (("X", lands),)

        def step0(self):
            self.go("A", ("P", "A-"), ("M", "A+"), ("X", "B"))

        def step1(self):
            self.wait("B")
            self.go("B", ("P", "B-"), ("M", "B+"))

        def step2(self):
            self.wait("A-")
            self.go("A-", ("P", "A--"), *self.across("C-"))
            self.wait("A+")
            self.go("A+", *self.across("C+"))

        def step3(self):
            self.wait("B+")
            self.go("B+", ("M", "B++"))
            self.wait("B-")
            self.go("B-")
            if self.split is not None:
                self.wait("C-")
                self.go("C-")
                self.wait("C+")
                self.go("C+")

        def step4(self):
            self.wait("A--")
            self.go("A--", *self.across("C--"))
            self.wait("B++")
            self.go("B++")

        def step5(self):
            self.wait("C--")
            self.go("C--")

        def siblings(self, *items):
            for item in items:
                self.wait("S" + item)

        def drain(self):
            for sent in self.sent:
                self.copy(*sent).wait_send()

    def half_slot(buffer):
        def slot(dy, dx, flip=False, rows=None):
            low, high = rows or (0, 128)
            chunk = ((y + dy + 4) % 4) * 2 + (xl + dx) % 2
            half = (1 - core) if flip else core
            return buffer.at[chunk, pl.ds(pl.multiple_of(half * 128 + low, 16), high - low), :]
        return slot

    def row_slot(dz, dx, **_):
        return rows.at[((z + 8 + dz - y) % 4) * 2 + (xh + dx) % 2]

    def row_part(q):
        return lambda dz, dx, **_: row_slot(dz, dx).at[:, pl.ds(q * 512, 512)]

    seq_ring = (seq_peer(s + 2 - 4 * xl), seq_peer((s + 4) % 16), seq_peer((s + 12) % 16), seq_peer(s + 1 - 2 * core))
    c_ring = Ring(half_slot(cols), c_send, c_recv, *seq_ring, split=80)
    p_ring = Ring(half_slot(panel), p_send, p_recv, *seq_ring)
    z_ring = (tensor_peer(t + 1 - 2 * xh), tensor_peer((t + 2) % 8), tensor_peer((t + 6) % 8), None)
    r_ring = [Ring(row_part(q), r_send.at[q], r_recv.at[q], *z_ring) for q in range(2)]

    for d in range(1, 8):
        there = panel_piece((t + 8 - d) % 8)
        remote(there, there, ag_send.at[d], ag_recv.at[d], across(d)).wait_recv()
    p_ring.step0()

    for copy in tt:
        copy.wait_recv()
    total = trace_own[...]
    for d in range(1, 8):
        total = total + trace_t[d]
    trace_sum[...] = total
    ts = exchange(16, lambda d: trace_sum, lambda d: trace_s.at[d], ts_send, ts_recv, along)
    relay_on(1)
    p_ring.step1()
    p_ring.step2()
    p_ring.step3()
    c_ring.step0()
    landed_rows(0)
    r_ring[0].step0()
    p_ring.step4()
    landed_rows(1)
    r_ring[1].step0()
    p_ring.siblings("A", "B", "A-", "A+", "B-", "B+", "A--", "B++")

    for copy in ts:
        copy.wait_recv()
    total = trace_sum[...]
    for d in range(1, 16):
        total = total + trace_s[d]
    shift = DAMPING * (jnp.sum(total) / TOKENS) / D

    def fill(b, _):
        at = pl.ds(pl.multiple_of(b * 128, 128), 128)
        block = jnp.zeros((128, 512), F32)
        for k in range(8):
            block = block + dot(panel[k, :, at], panel[k], ((0,), (0,)))
        eye = (
            b * 128 + lax.broadcasted_iota(jnp.int32, (128, 512), 0)
            == lax.broadcasted_iota(jnp.int32, (128, 512), 1)
        )
        ext[at, 0:512] = block * (1.0 / TOKENS) + jnp.where(eye, shift, 0.0)
        ext[at, 512:1024] = jnp.where(eye, 1.0, 0.0)
        return 0

    lax.fori_loop(0, 4, fill, 0)
    c_ring.step1()

    far = (y + 2) % 4
    apart = (z + 8 - 2 * y) % 4
    early = [(far + jnp.where(apart >= 2, 1, 2)) % 4, (far + jnp.where(apart == 3, 2, 3)) % 4]
    late = [far, (far + jnp.where(apart == 0, 1, apart)) % 4]

    def row_band(k, band):
        return jnp.concatenate([rows[k, 0, band, :], rows[k, 1, band, :]], axis=1)

    def product(chunks, band, right_of):
        total = None
        for ky in chunks:
            for kx in range(2):
                k = ky * 2 + kx
                term = dot(row_band(k, band), right_of(k), ((1,), (0,)))
                total = term if total is None else total + term
        return total

    def gram_band(chunks, band):
        for n in range(4):
            lanes = slice(n * 512, (n + 1) * 512)
            yield lanes, product(chunks, band, lambda k: cols[k, :, lanes])

    def factor(b):
        base = b * 128
        at = pl.ds(pl.multiple_of(base, 128), 128)
        tiles = [ext[pl.ds(pl.multiple_of(base + 8 * g, 8), 8), at] for g in range(16)]
        inv = jnp.concatenate(inverse_factor(tiles), axis=0)
        upper = dot_split(inv, ext[at, :], ((1,), (0,)))
        inverse[at, :] = upper[:, 512:1024]
        above[...] = upper

        def below(k, _):
            lanes = pl.ds(pl.multiple_of(k * 128, 128), 128)
            ext[lanes, :] = ext[lanes, :] - dot_split(above[:, lanes], above[...], ((0,), (0,)))
            return 0

        lax.fori_loop(b + 1, 4, below, 0)

    def factor_and_forward(b, _):
        factor(b)

        @pl.when(b == 0)
        def _():
            r_ring[0].step1()
            c_ring.step2()
            r_ring[0].step2()

        @pl.when(b == 1)
        def _():
            r_ring[1].step1()
            c_ring.step3()
            r_ring[1].step2()
            r_ring[0].step3()

        @pl.when(b == 2)
        def _():
            r_ring[1].step3()
            c_ring.step4()

        @pl.when(b == 3)
        def _():
            c_ring.step5()

        return 0

    lax.fori_loop(0, 4, factor_and_forward, 0)
    c_ring.siblings("A", "B", "A-", "A+", "B-", "B+", "C-", "C+")

    @pl.loop(0, 1024 // BAND)
    def _(m):
        band = pl.ds(pl.multiple_of(m * BAND, BAND), BAND)
        right[band, :] = product(early, band, lambda k: panel[k])
        for lanes, value in gram_band(early, band):
            gram[band, lanes] = value

    for ring in r_ring:
        ring.wait("A--")
        ring.wait("B++")

    @pl.loop(0, 1024 // BAND)
    def _(m):
        band = pl.ds(pl.multiple_of(m * BAND, BAND), BAND)
        at = s * 1024 + m * BAND - start
        eye = at + lax.broadcasted_iota(jnp.int32, (BAND, 512), 0) == lax.broadcasted_iota(jnp.int32, (BAND, 512), 1)
        block = right[band, :] + product(late, band, lambda k: panel[k]) + jnp.where(eye, shift, 0.0)
        white[band, :] = dot_split(block, inverse[...], ((1,), (1,))).astype(BF16)

    fetch[2].wait()
    for k in range(4):
        lanes = slice(k * 128, (k + 1) * 128)
        part[lanes, :] = dot(white[:, lanes], weight[...], ((0,), (1,))).astype(BF16)

    def part_rows(k):
        return part.at[pl.ds(pl.multiple_of(k * 32, 32), 32)]

    fs = exchange(16, lambda d: part_rows((s + d) % 16), lambda d: landed.at[d], f_send, f_recv, along)
    c_ring.siblings("A--", "B++", "C--")

    @pl.loop(0, 1024 // BAND)
    def _(m):
        band = pl.ds(pl.multiple_of(m * BAND, BAND), BAND)
        for lanes, value in gram_band(late, band):
            gram[band, lanes] = gram[band, lanes] + value

    @pl.when(i == t)
    def _():
        @pl.loop(0, 8)
        def _(m):
            band = pl.ds(pl.multiple_of(m * 128, 128), 128)
            at = pl.ds(pl.multiple_of(core * 1024 + m * 128, 128), 128)
            eye = lax.broadcasted_iota(jnp.int32, (128, 128), 0) == lax.broadcasted_iota(jnp.int32, (128, 128), 1)
            gram[band, at] += jnp.where(eye, shift, 0.0)

    for copy in fs:
        copy.wait_recv()
    total = part[pl.ds(pl.multiple_of(s * 32, 32), 32), :].astype(F32)
    for d in range(1, 16):
        total = total + landed[d].astype(F32)
    proj_out[...] = total

    for copies in (sq, rs, gt, tt, ag, ts, fs):
        for copy in copies:
            copy.wait_send()
    for ring in (p_ring, c_ring, *r_ring):
        ring.drain()
    for c in range(2):
        @pl.when(jnp.logical_not(jnp.logical_and(own, core == c)))
        def _():
            for q in range(2):
                into_rows(c, q, flipped).wait_send()

        @pl.when(y != 0)
        def _():
            to_shifted(c, 1).wait_send()

    @pl.when(y != 0)
    def _():
        gain_to_shifted().wait_send()


def on_device(tokens, norm_gain, projection_weight, panel_index):
    vmem = pl.BlockSpec(memory_space=pltpu.VMEM)
    hbm = pl.BlockSpec(memory_space=pltpu.HBM)
    dma = pltpu.SemaphoreType.DMA
    gram, white, projected = pl.pallas_call(
        kernel,
        out_shape=(
            jax.ShapeDtypeStruct((1024, 2048), F32),
            jax.ShapeDtypeStruct((1024, 512), BF16),
            jax.ShapeDtypeStruct((32, 256), F32),
        ),
        in_specs=[hbm, hbm, pl.BlockSpec(memory_space=pltpu.SMEM), hbm],
        out_specs=(vmem, vmem, vmem),
        scratch_shapes=[
            pltpu.VMEM((128, 2048), BF16),
            pltpu.VMEM((1, 2048), F32),
            pltpu.VMEM((256, 1024), BF16),
            pltpu.VMEM((8, 256, 2048), BF16),
            pltpu.VMEM((8, 2, 1024, 128), BF16),
            pltpu.VMEM((8, 256, 512), BF16),
            pltpu.VMEM((512, 1024), F32),
            pltpu.VMEM((512, 512), F32),
            pltpu.VMEM((512, 256), BF16),
            pltpu.VMEM((16, 32, 256), BF16),
            pltpu.VMEM((2048, 128), BF16),
            pltpu.VMEM((8, 8, 128), F32),
            pltpu.VMEM((128, 512), BF16),
            pltpu.VMEM((8, 16, 512), BF16),
            pltpu.VMEM((8, 512), F32),
            pltpu.VMEM((8, 8, 512), F32),
            pltpu.VMEM((128, 128), F32),
            pltpu.VMEM((8, 128), F32),
            pltpu.VMEM((8, 8, 128), F32),
            pltpu.VMEM((16, 8, 128), F32),
            pltpu.VMEM((8, 128), F32),
            dma((3,)),
            dma((8,)), dma((8,)), dma((8,)), dma((8,)), dma((8,)), dma((8,)),
            dma((8,)), dma((8,)), dma((8,)), dma((8,)), dma((16,)), dma((16,)),
            dma((22,)), dma((22,)), dma((22,)), dma((22,)), dma((2, 22)), dma((2, 22)), dma((4,)), dma((4,)), dma((2,)), dma((5,)), dma((5,)),
            pltpu.VMEM((2048, 128), BF16), pltpu.VMEM((1, 2048), F32), pltpu.VMEM((8, 128), F32),
            pltpu.VMEM((1024, 512), F32), pltpu.VMEM((128, 1024), F32), dma((16,)), dma((16,)),
        ],
        compiler_params=pltpu.CompilerParams(
            collective_id=0, has_side_effects=True, vmem_limit_bytes=36 * 1024 * 1024
        ),
        cost_estimate=pl.CostEstimate(flops=12_000_000_000, bytes_accessed=20_000_000, transcendentals=0),
        name="whiten",
    )(tokens, norm_gain[None, :], panel_index, projection_weight)
    return gram, white, projected.T


def solution(mesh):
    placed = (P("seq", "tensor"), P("tensor"), P("tensor", "seq"), P())
    return jax.shard_map(
        on_device,
        mesh=mesh,
        in_specs=placed,
        out_specs=(P("seq", "tensor"), P("seq", None), P("tensor", "seq")),
        check_vma=False,
    )
```
